32 devices in a mesh: gx: 8 (over z, x), gy: 4 (over y, core).
Axes of the slice: x: 2, y: 2, z: 4, core: 2. Of those that a mesh axis runs over, the one named last changes fastest.
Arguments:
- polar: float32 [512, 3072], P('gx', 'gy'), may hold values from -3.140625 to 3.140625
- azimuth: float32 [512, 3072], P('gx', 'gy'), may hold values from -3.140625 to 3.140625
- grains: int32 [512, 3072], P('gx', 'gy'), may hold values from 0 to 255, as said below
- stiffness: float32 [256], replicated, may hold values from 0.5 to 2
- anisotropy: float32 [256], replicated, may hold values from 0.2 to 2
- axis_polar: float32 [256], replicated, may hold values from -3.140625 to 3.140625
- axis_azimuth: float32 [256], replicated, may hold values from -3.140625 to 3.140625
- applied_field: float32 [3], replicated, may hold values from -3 to 3
Outputs:
- moment: float32 [3, 512, 3072], P(None, 'gx', 'gy')
- spin_flip: float32 [512, 256], P(('gx', 'gy'))
- non_flip: float32 [512, 256], P(('gx', 'gy'))
The draws below stay inside these ranges and needn't reach their ends.
Inputs may be any that keep to these rules, and one draw needn't show every extreme that they name: `grains`: grain label of each cell, a row of the grain tables.
All inputs are finite; a program needn't handle non-finite values.
Results may differ from the reference program's by a relative error of at most 0.0003.
Values sent between devices are 32-bit elements; how exact they have to be, the bound alone decides.
A program may use at most 128 MiB of HBM per device.

```python
import math
import jax
import jax.numpy as jnp
from jax import lax

NZ = 12
STEPS = 4
NGRAIN = 256
NX = 512
NY = 256


def grain_index(key, length):
    bits = jax.random.randint(key, (length,), 0, 2).astype(jnp.int32)
    start = jnp.zeros((1,), jnp.int32)
    return jnp.concatenate([start, jnp.cumsum(bits[:-1]).astype(jnp.int32)])


def draw_grains(key, part):
    key_x, key_y, key_z, key_label = jax.random.split(key, 4)
    index_x = grain_index(key_x, NX)
    index_y = grain_index(key_y, NY)
    index_z = grain_index(key_z, NZ)
    labels = jax.random.randint(key_label, (NX, NY, NZ), 0, NGRAIN).astype(jnp.int32)
    fine = labels[index_x[:, None, None], index_y[None, :, None], index_z[None, None, :]]
    return fine.reshape(NX, NY * NZ).astype(jnp.int32)


def bell_draw(own_key, shape, scale, reach, kind=jnp.bfloat16):
    entries = scale * jax.random.normal(own_key, shape, jnp.float32)
    return jnp.clip(entries, min=-reach, max=reach).astype(kind)


def setup_inputs(seed: int = 0) -> dict:
    key_list = jax.random.split(jax.random.key(seed), 9)
    polar = jnp.clip(jax.random.uniform(key_list[0], (NX, NY * NZ), jnp.float32, -3.140625, 3.140625), -3.140625, 3.140625)
    azimuth = jnp.clip(jax.random.uniform(key_list[1], (NX, NY * NZ), jnp.float32, -3.140625, 3.140625), -3.140625, 3.140625)
    grains = draw_grains(jax.random.fold_in(key_list[8], 71), 0)
    stiffness = jnp.clip(jnp.exp(jax.random.uniform(key_list[3], (NGRAIN,), jnp.float32, math.log(0.5), math.log(2.0))), 0.5, 2.0)
    anisotropy = jnp.clip(jnp.exp(jax.random.uniform(key_list[4], (NGRAIN,), jnp.float32, math.log(0.2), math.log(2.0))), 0.2, 2.0)
    axis_polar = jnp.clip(jax.random.uniform(key_list[5], (NGRAIN,), jnp.float32, -3.140625, 3.140625), -3.140625, 3.140625)
    axis_azimuth = jnp.clip(jax.random.uniform(key_list[6], (NGRAIN,), jnp.float32, -3.140625, 3.140625), -3.140625, 3.140625)
    applied_field = bell_draw(key_list[7], (3,), 0.5, 3.0, jnp.float32)
    return dict(polar=polar, azimuth=azimuth, grains=grains, stiffness=stiffness, anisotropy=anisotropy, axis_polar=axis_polar, axis_azimuth=axis_azimuth, applied_field=applied_field)


damping = 0.5
time_step = 0.12

def couple(left, right):
    return 2.0 * left * right / (left + right)

def cross(first, second):
    return jnp.stack([first[1] * second[2] - first[2] * second[1], first[2] * second[0] - first[0] * second[2], first[0] * second[1] - first[1] * second[0]])

def advance(center, plus_x, minus_x, plus_y, minus_y, weight, weight_px, weight_mx, weight_py, weight_my, strength, easy_axis, applied):
    field = couple(weight, weight_px) * (plus_x - center) + couple(weight, weight_mx) * (minus_x - center)
    field = field + couple(weight, weight_py) * (plus_y - center) + couple(weight, weight_my) * (minus_y - center)
    flux = couple(weight[1:], weight[:-1]) * (center[:, 1:] - center[:, :-1])
    zeros = jnp.zeros_like(center[:, :1])
    field = field + jnp.concatenate([flux, zeros], axis=1) - jnp.concatenate([zeros, flux], axis=1)
    project = easy_axis[0] * center[0] + easy_axis[1] * center[1] + easy_axis[2] * center[2]
    field = field + strength * project * easy_axis + applied.reshape(3, 1, 1, 1)
    torque = cross(center, field)
    damped = cross(center, torque)
    moved = center - time_step / (1.0 + damping * damping) * (torque + damping * damped)
    return moved / jnp.sqrt(moved[0] * moved[0] + moved[1] * moved[1] + moved[2] * moved[2])

def cross_sections(real_part, imag_part, wave_x, wave_y):
    squared = wave_x * wave_x + wave_y * wave_y
    inverse = 1.0 / jnp.sqrt(jnp.maximum(squared, 1.0))
    beam_stop = jnp.where(squared > 0.5, 1.0, 0.0).astype(real_part.dtype)
    unit_x = wave_x * inverse
    unit_y = wave_y * inverse
    pieces = []
    for part in (real_part, imag_part):
        along = unit_x * part[0] + unit_y * part[1]
        pieces.append((part[0] - unit_x * along, part[1] - unit_y * along, part[2]))
    non_flip = pieces[0][0] * pieces[0][0] + pieces[1][0] * pieces[1][0]
    spin_flip = pieces[0][1] * pieces[0][1] + pieces[1][1] * pieces[1][1] + pieces[0][2] * pieces[0][2] + pieces[1][2] * pieces[1][2]
    return (spin_flip * beam_stop, non_flip * beam_stop)

def signed_waves(length):
    counter = jnp.arange(length, dtype=jnp.int32)
    return jnp.where(counter < length // 2, counter, counter - length).astype(jnp.float32)

def to_volume(array):
    return jnp.transpose(array.reshape(NX, NY, NZ), (2, 0, 1))

def reference(polar, azimuth, grains, stiffness, anisotropy, axis_polar, axis_azimuth, applied_field):
    polar = to_volume(polar)
    azimuth = to_volume(azimuth)
    grains = to_volume(grains)
    moment = jnp.stack([jnp.sin(polar) * jnp.cos(azimuth), jnp.sin(polar) * jnp.sin(azimuth), jnp.cos(polar)])
    weight = stiffness[grains]
    strength = anisotropy[grains]
    easy_x = jnp.sin(axis_polar) * jnp.cos(axis_azimuth)
    easy_y = jnp.sin(axis_polar) * jnp.sin(axis_azimuth)
    easy_z = jnp.cos(axis_polar)
    easy_axis = jnp.stack([easy_x[grains], easy_y[grains], easy_z[grains]])
    weight_px = jnp.roll(weight, -1, axis=1)
    weight_mx = jnp.roll(weight, 1, axis=1)
    weight_py = jnp.roll(weight, -1, axis=2)
    weight_my = jnp.roll(weight, 1, axis=2)
    for turn_index in range(STEPS):
        moment = advance(moment, jnp.roll(moment, -1, axis=2), jnp.roll(moment, 1, axis=2), jnp.roll(moment, -1, axis=3), jnp.roll(moment, 1, axis=3), weight, weight_px, weight_mx, weight_py, weight_my, strength, easy_axis, applied_field)
    layer = lax.optimization_barrier(jnp.sum(moment, axis=1)) / math.sqrt(NZ)
    spectrum = jnp.fft.fft2(layer, axes=(1, 2))
    scale = math.sqrt(NX * NY)
    real_part = jnp.real(spectrum).astype(jnp.float32) / scale
    imag_part = jnp.imag(spectrum).astype(jnp.float32) / scale
    spin_flip, non_flip = cross_sections(real_part, imag_part, signed_waves(NX)[:, None], signed_waves(NY)[None, :])
    flat_moment = jnp.transpose(moment, (0, 2, 3, 1)).reshape(3, NX, NY * NZ)
    return (flat_moment, spin_flip, non_flip)
```

```python
import functools
import math

import jax
import jax.numpy as jnp
import numpy as np
from jax import lax
from jax.experimental import pallas as pl
from jax.experimental.pallas import tpu as pltpu
from jax.sharding import PartitionSpec as P
import ml_dtypes

NZ = 12
STEPS = 4
DAMPING = 0.5
TIME_STEP = 0.12
LANES = 128
SUB = 8
MESH = pl.DeviceIdType.MESH


def iota(shape, dim):
    return lax.broadcasted_iota(jnp.int32, shape, dim)


def sin_cos(x):
    turns = jnp.floor(x * (2.0 / math.pi) + 0.5)
    quadrant = turns.astype(jnp.int32)
    r = x - turns * 1.5703125
    r = r - turns * 4.837512969970703125e-4
    r = r - turns * 7.549789948768648e-8
    z = r * r
    sine = r + r * z * (-1.6666654611e-1 + z * (8.3321608736e-3 - z * 1.9515295891e-4))
    cosine = 1.0 - 0.5 * z + z * z * (
        4.166664568298827e-2 + z * (-1.388731625493765e-3 + z * 2.443315711809948e-5)
    )
    odd = (quadrant & 1) == 1
    s = jnp.where(odd, cosine, sine)
    c = jnp.where(odd, sine, cosine)
    s = jnp.where((quadrant & 2) == 2, -s, s)
    c = jnp.where(((quadrant + 1) & 2) == 2, -c, c)
    return s, c


def neighbours(ngx, ngy):
    gx, gy = lax.axis_index("gx"), lax.axis_index("gy")
    return (
        gx,
        gy,
        lax.rem(gx + 1, ngx),
        lax.rem(gx + ngx - 1, ngx),
        lax.rem(gy + 1, ngy),
        lax.rem(gy + ngy - 1, ngy),
    )


def halo_kernel(
    ngx, ngy, p_ref, a_ref, g_ref, rows_out, cols_out, corners_out,
    rows_msg, cols_msg, corners_msg, send, recv,
):
    gx, gy, down, up, right, left = neighbours(ngx, ngy)
    around = [
        (up, gy), (down, gy), (gx, left), (gx, right),
        (up, left), (up, right), (down, left), (down, right),
    ]
    barrier = pltpu.get_barrier_semaphore()
    for device in around:
        pl.semaphore_signal(barrier, inc=1, device_id=device, device_id_type=MESH)

    rows, columns = p_ref.shape
    half = columns // 2
    near = (slice(0, SUB), slice(rows - SUB, rows))
    side = (slice(0, LANES), slice(columns - LANES, columns))
    sub_low = iota((SUB, columns), 0) < 4
    for k in range(2):
        own = sub_low if k == 0 else jnp.logical_not(sub_low)
        g = g_ref[near[k], :].astype(jnp.float32)
        rows_msg[k, :, :columns] = jnp.where(
            own, p_ref[near[k], :], pltpu.roll(a_ref[near[k], :], 4, 0)
        )
        rows_msg[k, :, columns:] = jnp.where(
            own[:, :half], g[:, :half], pltpu.roll(g[:, half:], 4, 0)
        )
    lane_low = iota((rows, LANES), 1) < 64
    for k in range(2):
        own = lane_low if k == 0 else jnp.logical_not(lane_low)
        g = g_ref[:, side[k]].astype(jnp.float32)
        cols_msg[k, :rows] = jnp.where(own, p_ref[:, side[k]], pltpu.roll(a_ref[:, side[k]], 64, 1))
        cols_msg[k, rows:] = jnp.where(
            own[: rows // 2], g[: rows // 2], pltpu.roll(g[rows // 2 :], 64, 1)
        )
    tile_sub = iota((SUB, LANES), 0) < 4
    tile_lane = iota((SUB, LANES), 1) < 64
    for k in range(2):
        for j in range(2):
            own_sub = tile_sub if k == 0 else jnp.logical_not(tile_sub)
            own_lane = tile_lane if j == 0 else jnp.logical_not(tile_lane)
            g = g_ref[near[k], side[j]].astype(jnp.float32)
            corners_msg[2 * k + j] = jnp.where(
                own_sub,
                jnp.where(own_lane, p_ref[near[k], side[j]], pltpu.roll(a_ref[near[k], side[j]], 64, 1)),
                pltpu.roll(g, 4, 0),
            )
    pl.semaphore_wait(barrier, 8)
    sources = [rows_msg.at[0], rows_msg.at[1], cols_msg.at[0], cols_msg.at[1]]
    sources += [corners_msg.at[k] for k in range(4)]
    targets = [rows_out.at[0], rows_out.at[1], cols_out.at[0], cols_out.at[1]]
    targets += [corners_out.at[k] for k in range(4)]
    copies = [
        pltpu.make_async_remote_copy(
            src_ref=sources[k], dst_ref=targets[k], send_sem=send.at[k], recv_sem=recv.at[k],
            device_id=around[k], device_id_type=MESH,
        )
        for k in range(8)
    ]
    for copy in copies:
        copy.start()
    for copy in copies:
        copy.wait()


def halo(ngx, ngy, polar, azimuth, grains):
    rows, columns = polar.shape
    shapes = [(2, SUB, columns + columns // 2), (2, rows + rows // 2, LANES), (4, SUB, LANES)]
    vmem = pl.BlockSpec(memory_space=pltpu.VMEM)
    return pl.pallas_call(
        functools.partial(halo_kernel, ngx, ngy),
        out_shape=[jax.ShapeDtypeStruct(s, jnp.float32) for s in shapes],
        in_specs=[vmem] * 3,
        out_specs=[vmem] * 3,
        scratch_shapes=[pltpu.VMEM(s, jnp.float32) for s in shapes]
        + [pltpu.SemaphoreType.DMA((8,)), pltpu.SemaphoreType.DMA((8,))],
        compiler_params=pltpu.CompilerParams(
            collective_id=0, has_side_effects=True, vmem_limit_bytes=16 * 2**20
        ),
        name="halo",
    )(polar, azimuth, grains)


def steps_kernel(
    ngx, p_ref, a_ref, g_ref, rows_ref, cols_ref, corners_ref,
    stiff_ref, anis_ref, apol_ref, aazi_ref, applied_ref,
    moment_ref, layer_ref, m_ref, w_ref, coef_ref, axis_ref,
):
    rows, columns = p_ref.shape
    strips, tiles = rows // SUB, columns // LANES
    half = columns // 2
    lane = iota((SUB, LANES), 1)
    sub = iota((SUB, LANES), 0)
    sub_low, lane_low = sub < 4, lane < 64

    def raw(s, t):
        if s < strips and t < tiles:
            r, c = slice(s * SUB, s * SUB + SUB), slice(t * LANES, t * LANES + LANES)
            return p_ref[r, c], a_ref[r, c], g_ref[r, c]
        if s < strips:
            r = slice(s * SUB, s * SUB + SUB)
            k = (s * SUB) % (rows // 2) + rows
            rg = slice(k, k + SUB)
            fr, fl = cols_ref[0, r, :], cols_ref[1, r, :]
            gr, gl = cols_ref[0, rg, :], cols_ref[1, rg, :]
            p = jnp.where(lane_low, fr, fl)
            a = pltpu.roll(jnp.where(lane_low, fl, fr), 64, 1)
            if s * SUB < rows // 2:
                g = jnp.where(lane_low, gr, gl)
            else:
                g = pltpu.roll(jnp.where(lane_low, gl, gr), 64, 1)
        elif t < tiles:
            c = slice(t * LANES, t * LANES + LANES)
            k = (t * LANES) % half + columns
            cg = slice(k, k + LANES)
            fn, fp = rows_ref[0, :, c], rows_ref[1, :, c]
            gn, gp = rows_ref[0, :, cg], rows_ref[1, :, cg]
            p = jnp.where(sub_low, fn, fp)
            a = pltpu.roll(jnp.where(sub_low, fp, fn), 4, 0)
            if t * LANES < half:
                g = jnp.where(sub_low, gn, gp)
            else:
                g = pltpu.roll(jnp.where(sub_low, gp, gn), 4, 0)
        else:
            q = [corners_ref[k] for k in range(4)]
            p = jnp.where(sub_low, jnp.where(lane_low, q[0], q[1]), jnp.where(lane_low, q[2], q[3]))
            a = jnp.where(sub_low, jnp.where(lane_low, q[1], q[0]), jnp.where(lane_low, q[3], q[2]))
            a = pltpu.roll(a, 64, 1)
            g = jnp.where(sub_low, jnp.where(lane_low, q[2], q[3]), jnp.where(lane_low, q[0], q[1]))
            g = pltpu.roll(g, 4, 0)
        return p, a, g.astype(jnp.int32)

    def store(ref, lead, s, t, value):
        ref[(*lead, t, slice(SUB + s * SUB, 2 * SUB + s * SUB), slice(None))] = value
        if s == 0:
            k = SUB * (strips + 2)
            ref[(*lead, t, slice(k, k + SUB), slice(None))] = value
        if s == strips:
            ref[(*lead, t, slice(0, SUB), slice(None))] = value

    def rows_of(ref, lead, s, t, shift=0):
        k = SUB + s * SUB + shift
        return ref[(*lead, t, slice(k, k + SUB), slice(None))]

    sp, cp = sin_cos(apol_ref[...])
    sa, ca = sin_cos(aazi_ref[...])
    root = jnp.sqrt(anis_ref[...])
    tables = [stiff_ref[...], root * sp * ca, root * sp * sa, root * cp]
    pages = [
        [jnp.broadcast_to(table[:, k : k + LANES], (SUB, LANES)) for k in range(0, table.shape[1], LANES)]
        for table in tables
    ]

    for s in range(strips + 1):
        for t in range(tiles + 1):
            p, a, g = raw(s, t)
            sp, cp = sin_cos(p)
            sa, ca = sin_cos(a)
            for c, value in enumerate((sp * ca, sp * sa, cp)):
                store(m_ref, (0, c), s, t, value)
            place = g & (LANES - 1)
            page = g >> 7
            found = []
            for table in pages:
                value = jnp.take_along_axis(table[0], place, axis=1, mode="promise_in_bounds")
                for k in range(1, len(table)):
                    other = jnp.take_along_axis(table[k], place, axis=1, mode="promise_in_bounds")
                    value = jnp.where(page == k, other, value)
                found.append(value)
            store(w_ref, (), s, t, found[0])
            for c in range(3):
                axis_ref[c, t, s * SUB : s * SUB + SUB, :] = found[1 + c]

    count = tiles + 1

    def shifter(values, shift):
        turned = {}

        def turn(t):
            t = t % count
            if t not in turned:
                turned[t] = pltpu.roll(values[t], (-shift) % LANES, 1)
            return turned[t]

        def at(t):
            if shift > 0:
                return jnp.where(lane < LANES - shift, turn(t), turn(t + 1))
            return jnp.where(lane >= -shift, turn(t), turn(t - 1))

        return at

    def couple(p, q):
        return 2.0 * p * q / (p + q)

    for s in range(strips + 1):
        here = [rows_of(w_ref, (), s, t) for t in range(count)]
        plus_y = shifter(here, NZ)
        plus_z = shifter(here, 1)
        y_link = [couple(here[t], plus_y(t)) for t in range(count)]
        z_link = []
        for t in range(count):
            spot = t * LANES + lane
            if t == tiles:
                spot = jnp.where(lane_low, spot, spot - count * LANES + NZ * LANES)
            level = spot - NZ * ((spot * 43691) >> 19)
            z_link.append(jnp.where(level < NZ - 1, couple(here[t], plus_z(t)), 0.0))
        y_back = shifter(y_link, -NZ)
        z_back = shifter(z_link, -1)
        for t in range(count):
            links = [
                couple(here[t], rows_of(w_ref, (), s, t, 1)),
                couple(here[t], rows_of(w_ref, (), s, t, -1)),
                y_link[t],
                y_back(t),
                z_link[t],
                z_back(t),
            ]
            total = links[0] + links[1] + links[2] + links[3] + links[4] + links[5]
            for k, value in enumerate(links + [total]):
                coef_ref[k, t, s * SUB : s * SUB + SUB, :] = value

    applied = [applied_ref[c] for c in range(3)]
    factor = TIME_STEP / (1.0 + DAMPING * DAMPING)

    def one_step(index, carry):
        now = lax.rem(index, 2)
        later = 1 - now
        for s in range(strips + 1):
            here = [[rows_of(m_ref, (now, c), s, t) for t in range(count)] for c in range(3)]
            shifts = [[shifter(here[c], k) for k in (NZ, -NZ, 1, -1)] for c in range(3)]
            for t in range(count):
                spot = (t, slice(s * SUB, s * SUB + SUB), slice(None))
                link = [coef_ref[(k, *spot)] for k in range(7)]
                easy = [axis_ref[(c, *spot)] for c in range(3)]
                m = [here[c][t] for c in range(3)]
                project = easy[0] * m[0] + easy[1] * m[1] + easy[2] * m[2]
                h = []
                for c in range(3):
                    value = link[0] * rows_of(m_ref, (now, c), s, t, 1)
                    value = value + link[1] * rows_of(m_ref, (now, c), s, t, -1)
                    for k in range(4):
                        value = value + link[2 + k] * shifts[c][k](t)
                    value = value - link[6] * m[c]
                    h.append(value + project * easy[c] + applied[c])

                def cross(f, g):
                    return [
                        f[1] * g[2] - f[2] * g[1],
                        f[2] * g[0] - f[0] * g[2],
                        f[0] * g[1] - f[1] * g[0],
                    ]

                torque = cross(m, h)
                damped = cross(m, torque)
                moved = [
                    m[c] - (factor * torque[c] + (factor * DAMPING) * damped[c]) for c in range(3)
                ]
                size = moved[0] * moved[0] + moved[1] * moved[1] + moved[2] * moved[2]
                inverse = lax.rsqrt(size)
                for c in range(3):
                    store(m_ref, (later, c), s, t, moved[c] * inverse)
        return carry

    lax.fori_loop(0, STEPS, one_step, 0)

    last = STEPS % 2
    width_y = columns // NZ
    per = width_y // ngx
    row = iota((ngx * SUB, columns), 0)
    column = iota((ngx * SUB, columns), 1)
    cell = (row // SUB) * per + row % SUB
    inside = (column >= cell * NZ) & (column < cell * NZ + NZ) & (row % SUB < per)
    chooser = jnp.where(inside, 1.0, 0.0).astype(jnp.bfloat16)
    for c in range(3):
        for t in range(tiles):
            moment_ref[c, :, t * LANES : t * LANES + LANES] = m_ref[last, c, t, SUB : SUB + rows, :]
        whole = moment_ref[c]
        high = whole.astype(jnp.bfloat16)
        low = (whole - high.astype(jnp.float32)).astype(jnp.bfloat16)
        sums = sum(
            lax.dot_general(
                chooser, part, (((1,), (1,)), ((), ())), preferred_element_type=jnp.float32
            )
            for part in (low, high)
        )
        layer_ref[:, c * rows : c * rows + rows] = sums * (1.0 / math.sqrt(NZ))
    layer_ref[:, 3 * rows :] = jnp.zeros((ngx * SUB, rows), jnp.float32)


def steps(ngx, polar, azimuth, grains, ghosts, tables, applied):
    rows, columns = polar.shape
    vmem = pl.BlockSpec(memory_space=pltpu.VMEM)
    strips, tiles = rows // SUB + 1, columns // LANES + 1
    return pl.pallas_call(
        functools.partial(steps_kernel, ngx),
        out_shape=[
            jax.ShapeDtypeStruct((3, rows, columns), jnp.float32),
            jax.ShapeDtypeStruct((ngx * SUB, 4 * rows), jnp.float32),
        ],
        in_specs=[vmem] * 10 + [pl.BlockSpec(memory_space=pltpu.SMEM)],
        out_specs=[vmem] * 2,
        scratch_shapes=[
            pltpu.VMEM((2, 3, tiles, SUB * (strips + 2), LANES), jnp.float32),
            pltpu.VMEM((tiles, SUB * (strips + 2), LANES), jnp.float32),
            pltpu.VMEM((7, tiles, SUB * strips, LANES), jnp.float32),
            pltpu.VMEM((3, tiles, SUB * strips, LANES), jnp.float32),
        ],
        compiler_params=pltpu.CompilerParams(vmem_limit_bytes=32 * 2**20),
        name="steps",
    )(polar, azimuth, grains, *ghosts, *tables, applied)


def split(values):
    high = values.astype(ml_dtypes.bfloat16)
    low = (values - high.astype(np.float64)).astype(ml_dtypes.bfloat16)
    return high, low


def wave_tables(ngx, ngy, width_x, width_y):
    total_x, total_y = width_x * ngx, width_y * ngy
    devices = ngx * ngy
    per_x, per_y = width_x // ngy, width_y // ngx
    x = np.arange(total_x)
    angle = 2.0 * np.pi / total_x * (np.outer(x, x) % total_x)
    both = np.stack([np.cos(angle), -np.sin(angle)], axis=1).reshape(total_x, 2, devices, per_x)
    table_x = both.transpose(0, 2, 1, 3).reshape(total_x, 2 * total_x)
    y = np.arange(total_y)
    angle = 2.0 * np.pi / total_y * (np.outer(y, y) % total_y)
    both = np.concatenate([np.cos(angle), np.sin(angle)], axis=1)
    table_y = np.zeros((devices, SUB, 2 * total_y))
    table_y[:, :per_y] = both.reshape(devices, per_y, 2 * total_y)
    return (*split(table_x), *split(table_y.reshape(devices * SUB, 2 * total_y)))


def two_parts(value):
    high = value.astype(jnp.bfloat16).astype(jnp.float32)
    return jnp.concatenate([high, value - high], axis=0).astype(jnp.bfloat16)


def product(value, high_ref, low_ref):
    rows = value.shape[0]
    parts = two_parts(value)
    big = jnp.dot(parts, high_ref[...], preferred_element_type=jnp.float32)
    head = -(-rows // 16) * 16
    small = jnp.dot(parts[:head], low_ref[...], preferred_element_type=jnp.float32)
    return (big[rows:] + small[:rows]) + big[:rows]


def waves_kernel(
    ngx, ngy, layer_ref, xh_hbm, xl_hbm, yh_hbm, yl_hbm, flip_ref, non_ref,
    xh, xl, yh, yl, lines, message, held, load, send_x, recv_x, send_y, recv_y,
):
    gx, gy = lax.axis_index("gx"), lax.axis_index("gy")
    devices = ngx * ngy
    me = gx * ngy + gy
    width_x = layer_ref.shape[1] // 4
    total_x = ngx * width_x
    per_x = width_x // ngy
    total_y = yh.shape[1] // 2
    loads = [
        pltpu.make_async_copy(source, target, load.at[k])
        for k, (source, target) in enumerate([(xh_hbm, xh), (xl_hbm, xl), (yh_hbm, yh), (yl_hbm, yl)])
    ]
    barrier = pltpu.get_barrier_semaphore()

    def greet(k, carry):
        other = lax.rem(me + k, devices)
        pl.semaphore_signal(
            barrier, inc=1, device_id=(other // ngy, other % ngy), device_id_type=MESH
        )
        return carry

    lax.fori_loop(1, devices, greet, 0)
    for copy in loads:
        copy.start()
    pl.semaphore_wait(barrier, devices - 1)

    def line_copy(k):
        other = lax.rem(gx + k, ngx)
        source = lax.rem(gx + ngx - k, ngx)
        return pltpu.make_async_remote_copy(
            src_ref=layer_ref.at[pl.ds(pl.multiple_of(other * SUB, SUB), SUB)],
            dst_ref=lines.at[gx], send_sem=send_x.at[k], recv_sem=recv_x.at[k],
            device_id=(other, gy), device_id_type=MESH,
        )

    for k in range(1, ngx):
        line_copy(k).start()
    lines[gx] = layer_ref[pl.ds(pl.multiple_of(gx * SUB, SUB), SUB), :]
    for k in range(1, ngx):
        line_copy(k).wait()
    loads[0].wait()
    loads[1].wait()

    whole = jnp.concatenate(
        [
            jnp.concatenate(
                [lines[s, :, c * width_x : c * width_x + width_x] for s in range(ngx)], axis=1
            )
            for c in range(3)
        ],
        axis=0,
    )
    waves = product(whole, xh, xl)
    wide = 2 * per_x
    blank = jnp.zeros((SUB, LANES - 3 * wide), jnp.float32)
    for d in range(devices):
        pieces = [waves[c * SUB : c * SUB + SUB, d * wide : d * wide + wide] for c in range(3)]
        message[d] = jnp.concatenate(pieces + [blank], axis=1)

    slot = gy * ngx + gx

    def wave_copy(k):
        other = lax.rem(me + k, devices)
        return pltpu.make_async_remote_copy(
            src_ref=message.at[other], dst_ref=held.at[slot],
            send_sem=send_y.at[k], recv_sem=recv_y.at[k],
            device_id=(other // ngy, other % ngy), device_id_type=MESH,
        )

    def start(k, carry):
        wave_copy(k).start()
        return carry

    def finish(k, carry):
        wave_copy(k).wait()
        return carry

    lax.fori_loop(1, devices, start, 0)
    held[slot] = message[me]
    loads[2].wait()
    loads[3].wait()
    lax.fori_loop(1, devices, finish, 0)

    table = held[...].reshape(devices * SUB, LANES).T
    spectrum = product(table, yh, yl) * (1.0 / math.sqrt(total_x * total_y))

    counter_x = me * per_x + iota((per_x, total_y), 0)
    counter_y = iota((per_x, total_y), 1)
    wave_x = jnp.where(counter_x < total_x // 2, counter_x, counter_x - total_x).astype(jnp.float32)
    wave_y = jnp.where(counter_y < total_y // 2, counter_y, counter_y - total_y).astype(jnp.float32)
    squared = wave_x * wave_x + wave_y * wave_y
    inverse = 1.0 / jnp.sqrt(jnp.maximum(squared, 1.0))
    beam_stop = jnp.where(squared > 0.5, 1.0, 0.0)
    unit_x, unit_y = wave_x * inverse, wave_y * inverse
    real, imag = [], []
    for c in range(3):
        re = spectrum[c * wide : c * wide + per_x]
        im = spectrum[c * wide + per_x : c * wide + wide]
        real.append(re[:, :total_y] + im[:, total_y:])
        imag.append(im[:, :total_y] - re[:, total_y:])
    flip = jnp.zeros_like(squared)
    non = jnp.zeros_like(squared)
    for part in (real, imag):
        along = unit_x * part[0] + unit_y * part[1]
        first = part[0] - unit_x * along
        second = part[1] - unit_y * along
        non = non + first * first
        flip = flip + second * second + part[2] * part[2]
    flip_ref[...] = flip * beam_stop
    non_ref[...] = non * beam_stop


def waves(ngx, ngy, width_x, width_y, layer):
    tables = wave_tables(ngx, ngy, width_x, width_y)
    devices = ngx * ngy
    vmem = pl.BlockSpec(memory_space=pltpu.VMEM)
    out = jax.ShapeDtypeStruct((width_x // ngy, width_y * ngy), jnp.float32)
    return pl.pallas_call(
        functools.partial(waves_kernel, ngx, ngy),
        out_shape=[out, out],
        in_specs=[vmem] + [pl.BlockSpec(memory_space=pl.ANY)] * 4,
        out_specs=[vmem] * 2,
        scratch_shapes=[pltpu.VMEM(t.shape, jnp.bfloat16) for t in tables]
        + [
            pltpu.VMEM((ngx, SUB, 4 * width_x), jnp.float32),
            pltpu.VMEM((devices, SUB, LANES), jnp.float32),
            pltpu.VMEM((devices, SUB, LANES), jnp.float32),
            pltpu.SemaphoreType.DMA((4,)),
            pltpu.SemaphoreType.DMA((ngx,)),
            pltpu.SemaphoreType.DMA((ngx,)),
            pltpu.SemaphoreType.DMA((devices,)),
            pltpu.SemaphoreType.DMA((devices,)),
        ],
        compiler_params=pltpu.CompilerParams(
            collective_id=1, has_side_effects=True, vmem_limit_bytes=56 * 2**20
        ),
        name="waves",
    )(layer, *[jnp.asarray(t) for t in tables])


def solution(mesh):
    ngx, ngy = mesh.shape["gx"], mesh.shape["gy"]

    def shards(polar, azimuth, grains, stiffness, anisotropy, axis_polar, axis_azimuth, applied):
        width_x, width_y = polar.shape[0], polar.shape[1] // NZ
        ghosts = halo(ngx, ngy, polar, azimuth, grains)
        tables = [t.reshape(1, -1) for t in (stiffness, anisotropy, axis_polar, axis_azimuth)]
        moment, layer = steps(ngx, polar, azimuth, grains, ghosts, tables, applied)
        flip, non = waves(ngx, ngy, width_x, width_y, layer)
        return (moment, flip, non)

    in_specs = (P("gx", "gy"), P("gx", "gy"), P("gx", "gy"), P(), P(), P(), P(), P())
    out_specs = (P(None, "gx", "gy"), P(("gx", "gy"), None), P(("gx", "gy"), None))
    return jax.shard_map(shards, mesh=mesh, in_specs=in_specs, out_specs=out_specs, check_vma=False)
```

```python
import functools
import math

import jax
import jax.numpy as jnp
import numpy as np
from jax import lax
from jax.experimental import pallas as pl
from jax.experimental.pallas import tpu as pltpu
from jax.sharding import PartitionSpec as P
import ml_dtypes

NZ = 12
STEPS = 4
DAMPING = 0.5
TIME_STEP = 0.12
LANES = 128
SUB = 8
MESH = pl.DeviceIdType.MESH


def iota(shape, dim):
    return lax.broadcasted_iota(jnp.int32, shape, dim)


def sin_cos(x):
    turns = jnp.floor(x * (2.0 / math.pi) + 0.5)
    quadrant = turns.astype(jnp.int32)
    r = x - turns * 1.5703125
    r = r - turns * 4.837512969970703125e-4
    r = r - turns * 7.549789948768648e-8
    z = r * r
    sine = r + r * z * (-1.6666654611e-1 + z * (8.3321608736e-3 - z * 1.9515295891e-4))
    cosine = 1.0 - 0.5 * z + z * z * (
        4.166664568298827e-2 + z * (-1.388731625493765e-3 + z * 2.443315711809948e-5)
    )
    odd = (quadrant & 1) == 1
    s = jnp.where(odd, cosine, sine)
    c = jnp.where(odd, sine, cosine)
    s = jnp.where((quadrant & 2) == 2, -s, s)
    c = jnp.where(((quadrant + 1) & 2) == 2, -c, c)
    return s, c


def wrap(value, count):
    return jnp.where(value >= count, value - count, value)


def for_others(ngx, ngy, gx, gy, act):
    def row(i, first):
        other_x = wrap(gx + i, ngx)
        for j in range(first, ngy):
            act(other_x, wrap(gy + j, ngy))

    def turn(i, carry):
        row(i, 0)
        return carry

    row(0, 1)
    lax.fori_loop(1, ngx, turn, 0)


def split(values):
    high = values.astype(ml_dtypes.bfloat16)
    low = (values - high.astype(np.float64)).astype(ml_dtypes.bfloat16)
    return high, low


def wave_tables(ngx, ngy, width_x, width_y):
    total_x, total_y = width_x * ngx, width_y * ngy
    devices = ngx * ngy
    per_x, per_y = width_x // ngy, width_y // ngx
    x = np.arange(total_x)
    angle = 2.0 * np.pi / total_x * (np.outer(x, x) % total_x)
    both = np.stack([np.cos(angle), -np.sin(angle)], axis=1).reshape(total_x, 2, devices, per_x)
    table_x = both.transpose(0, 2, 1, 3).reshape(total_x, 2 * total_x)
    y = np.arange(total_y)
    angle = 2.0 * np.pi / total_y * (np.outer(y, y) % total_y)
    both = np.concatenate([np.cos(angle), np.sin(angle)], axis=1)
    table_y = np.zeros((devices, SUB, 2 * total_y))
    table_y[:, :per_y] = both.reshape(devices, per_y, 2 * total_y)
    return (*split(table_x), *split(table_y.reshape(devices * SUB, 2 * total_y)))


def two_parts(value):
    high = value.astype(jnp.bfloat16).astype(jnp.float32)
    return jnp.concatenate([high, value - high], axis=0).astype(jnp.bfloat16)


def product(value, high_ref, low_ref):
    rows = value.shape[0]
    parts = two_parts(value)
    big = jnp.dot(parts, high_ref[...], preferred_element_type=jnp.float32)
    head = -(-rows // 16) * 16
    small = jnp.dot(parts[:head], low_ref[...], preferred_element_type=jnp.float32)
    return (big[rows:] + small[:rows]) + big[:rows]


def main_kernel(
    ngx, ngy, p_hbm, a_hbm, g_hbm, xh_hbm, xl_hbm, yh_hbm, yl_hbm,
    stiff_ref, anis_ref, apol_ref, aazi_ref, applied_ref, moment_hbm, spectrum_ref,
    p_ref, a_ref, g_ref, xh, xl, yh, yl,
    rows_msg, cols_msg, corners_msg, rows_out, cols_out, corners_out,
    m_ref, w_ref, coef_ref, axis_ref, moment_ref, layer_ref, lines, message, held,
    load, send, recv, send_x, recv_x, send_y, recv_y,
):
    devices = ngx * ngy
    gx, gy = lax.axis_index("gx"), lax.axis_index("gy")
    down, up = wrap(gx + 1, ngx), wrap(gx + ngx - 1, ngx)
    right, left = wrap(gy + 1, ngy), wrap(gy + ngy - 1, ngy)
    around = [
        (up, gy), (down, gy), (gx, left), (gx, right),
        (up, left), (up, right), (down, left), (down, right),
    ]
    pairs = [
        (p_hbm, p_ref), (a_hbm, a_ref), (g_hbm, g_ref),
        (xh_hbm, xh), (xl_hbm, xl), (yh_hbm, yh), (yl_hbm, yl),
    ]
    loads = [pltpu.make_async_copy(s, t, load.at[k]) for k, (s, t) in enumerate(pairs)]
    for copy in loads[:3]:
        copy.start()
    barrier = pltpu.get_barrier_semaphore()

    def greet(other_x, other_y):
        pl.semaphore_signal(barrier, inc=1, device_id=(other_x, other_y), device_id_type=MESH)

    for_others(ngx, ngy, gx, gy, greet)
    for copy in loads[:3]:
        copy.wait()

    rows, columns = p_ref.shape
    half = columns // 2
    near = (slice(0, SUB), slice(rows - SUB, rows))
    side = (slice(0, LANES), slice(columns - LANES, columns))
    sub_low = iota((SUB, columns), 0) < 4
    for k in range(2):
        own = sub_low if k == 0 else jnp.logical_not(sub_low)
        g = g_ref[near[k], :].astype(jnp.float32)
        rows_msg[k, :, :columns] = jnp.where(
            own, p_ref[near[k], :], pltpu.roll(a_ref[near[k], :], 4, 0)
        )
        rows_msg[k, :, columns:] = jnp.where(
            own[:, :half], g[:, :half], pltpu.roll(g[:, half:], 4, 0)
        )
    lane_low = iota((rows, LANES), 1) < 64
    for k in range(2):
        own = lane_low if k == 0 else jnp.logical_not(lane_low)
        g = g_ref[:, side[k]].astype(jnp.float32)
        cols_msg[k, :rows] = jnp.where(own, p_ref[:, side[k]], pltpu.roll(a_ref[:, side[k]], 64, 1))
        cols_msg[k, rows:] = jnp.where(
            own[: rows // 2], g[: rows // 2], pltpu.roll(g[rows // 2 :], 64, 1)
        )
    tile_sub = iota((SUB, LANES), 0) < 4
    tile_lane = iota((SUB, LANES), 1) < 64
    for k in range(2):
        for j in range(2):
            own_sub = tile_sub if k == 0 else jnp.logical_not(tile_sub)
            own_lane = tile_lane if j == 0 else jnp.logical_not(tile_lane)
            g = g_ref[near[k], side[j]].astype(jnp.float32)
            corners_msg[2 * k + j] = jnp.where(
                own_sub,
                jnp.where(own_lane, p_ref[near[k], side[j]], pltpu.roll(a_ref[near[k], side[j]], 64, 1)),
                pltpu.roll(g, 4, 0),
            )
    pl.semaphore_wait(barrier, devices - 1)
    sources = [rows_msg.at[0], rows_msg.at[1], cols_msg.at[0], cols_msg.at[1]]
    sources += [corners_msg.at[k] for k in range(4)]
    targets = [rows_out.at[0], rows_out.at[1], cols_out.at[0], cols_out.at[1]]
    targets += [corners_out.at[k] for k in range(4)]
    copies = [
        pltpu.make_async_remote_copy(
            src_ref=sources[k], dst_ref=targets[k], send_sem=send.at[k], recv_sem=recv.at[k],
            device_id=around[k], device_id_type=MESH,
        )
        for k in range(8)
    ]
    for copy in copies:
        copy.start()
    for copy in loads[3:]:
        copy.start()

    strips, tiles = rows // SUB, columns // LANES
    lane = iota((SUB, LANES), 1)
    sub = iota((SUB, LANES), 0)
    sub_low, lane_low = sub < 4, lane < 64

    def raw(s, t):
        if s < strips and t < tiles:
            r, c = slice(s * SUB, s * SUB + SUB), slice(t * LANES, t * LANES + LANES)
            return p_ref[r, c], a_ref[r, c], g_ref[r, c]
        if s < strips:
            r = slice(s * SUB, s * SUB + SUB)
            k = (s * SUB) % (rows // 2) + rows
            rg = slice(k, k + SUB)
            fr, fl = cols_out[0, r, :], cols_out[1, r, :]
            gr, gl = cols_out[0, rg, :], cols_out[1, rg, :]
            p = jnp.where(lane_low, fr, fl)
            a = pltpu.roll(jnp.where(lane_low, fl, fr), 64, 1)
            if s * SUB < rows // 2:
                g = jnp.where(lane_low, gr, gl)
            else:
                g = pltpu.roll(jnp.where(lane_low, gl, gr), 64, 1)
        elif t < tiles:
            c = slice(t * LANES, t * LANES + LANES)
            k = (t * LANES) % half + columns
            cg = slice(k, k + LANES)
            fn, fp = rows_out[0, :, c], rows_out[1, :, c]
            gn, gp = rows_out[0, :, cg], rows_out[1, :, cg]
            p = jnp.where(sub_low, fn, fp)
            a = pltpu.roll(jnp.where(sub_low, fp, fn), 4, 0)
            if t * LANES < half:
                g = jnp.where(sub_low, gn, gp)
            else:
                g = pltpu.roll(jnp.where(sub_low, gp, gn), 4, 0)
        else:
            q = [corners_out[k] for k in range(4)]
            p = jnp.where(sub_low, jnp.where(lane_low, q[0], q[1]), jnp.where(lane_low, q[2], q[3]))
            a = jnp.where(sub_low, jnp.where(lane_low, q[1], q[0]), jnp.where(lane_low, q[3], q[2]))
            a = pltpu.roll(a, 64, 1)
            g = jnp.where(sub_low, jnp.where(lane_low, q[2], q[3]), jnp.where(lane_low, q[0], q[1]))
            g = pltpu.roll(g, 4, 0)
        return p, a, g.astype(jnp.int32)

    def store(ref, lead, s, t, value):
        ref[(*lead, t, slice(SUB + s * SUB, 2 * SUB + s * SUB), slice(None))] = value
        if s == 0:
            k = SUB * (strips + 2)
            ref[(*lead, t, slice(k, k + SUB), slice(None))] = value
        if s == strips:
            ref[(*lead, t, slice(0, SUB), slice(None))] = value

    def rows_of(ref, lead, s, t, shift=0):
        k = SUB + s * SUB + shift
        return ref[(*lead, t, slice(k, k + SUB), slice(None))]

    sp, cp = sin_cos(apol_ref[...])
    sa, ca = sin_cos(aazi_ref[...])
    root = jnp.sqrt(anis_ref[...])
    tables = [stiff_ref[...], root * sp * ca, root * sp * sa, root * cp]
    pages = [
        [jnp.broadcast_to(table[:, k : k + LANES], (SUB, LANES)) for k in range(0, table.shape[1], LANES)]
        for table in tables
    ]

    def prepare(s, t):
        p, a, g = raw(s, t)
        sp, cp = sin_cos(p)
        sa, ca = sin_cos(a)
        for c, value in enumerate((sp * ca, sp * sa, cp)):
            store(m_ref, (0, c), s, t, value)
        place = g & (LANES - 1)
        page = g >> 7
        found = []
        for table in pages:
            value = jnp.take_along_axis(table[0], place, axis=1, mode="promise_in_bounds")
            for k in range(1, len(table)):
                other = jnp.take_along_axis(table[k], place, axis=1, mode="promise_in_bounds")
                value = jnp.where(page == k, other, value)
            found.append(value)
        store(w_ref, (), s, t, found[0])
        for c in range(3):
            axis_ref[c, t, s * SUB : s * SUB + SUB, :] = found[1 + c]

    for s in range(strips):
        for t in range(tiles):
            prepare(s, t)
    for copy in copies:
        copy.wait()
    for s in range(strips + 1):
        for t in range(tiles + 1):
            if s == strips or t == tiles:
                prepare(s, t)

    count = tiles + 1

    def shifter(values, shift):
        turned = {}

        def turn(t):
            t = t % count
            if t not in turned:
                turned[t] = pltpu.roll(values[t], (-shift) % LANES, 1)
            return turned[t]

        def at(t):
            if shift > 0:
                return jnp.where(lane < LANES - shift, turn(t), turn(t + 1))
            return jnp.where(lane >= -shift, turn(t), turn(t - 1))

        return at

    def couple(p, q):
        return 2.0 * p * q / (p + q)

    for s in range(strips + 1):
        here = [rows_of(w_ref, (), s, t) for t in range(count)]
        plus_y = shifter(here, NZ)
        plus_z = shifter(here, 1)
        y_link = [couple(here[t], plus_y(t)) for t in range(count)]
        z_link = []
        for t in range(count):
            spot = t * LANES + lane
            if t == tiles:
                spot = jnp.where(lane_low, spot, spot - count * LANES + NZ * LANES)
            level = spot - NZ * ((spot * 43691) >> 19)
            z_link.append(jnp.where(level < NZ - 1, couple(here[t], plus_z(t)), 0.0))
        y_back = shifter(y_link, -NZ)
        z_back = shifter(z_link, -1)
        for t in range(count):
            links = [
                couple(here[t], rows_of(w_ref, (), s, t, 1)),
                couple(here[t], rows_of(w_ref, (), s, t, -1)),
                y_link[t],
                y_back(t),
                z_link[t],
                z_back(t),
            ]
            total = links[0] + links[1] + links[2] + links[3] + links[4] + links[5]
            for k, value in enumerate(links + [total]):
                coef_ref[k, t, s * SUB : s * SUB + SUB, :] = value

    applied = [applied_ref[c] for c in range(3)]
    factor = TIME_STEP / (1.0 + DAMPING * DAMPING)

    def one_step(index, carry):
        now = lax.rem(index, 2)
        later = 1 - now
        for s in range(strips + 1):
            here = [[rows_of(m_ref, (now, c), s, t) for t in range(count)] for c in range(3)]
            shifts = [[shifter(here[c], k) for k in (NZ, -NZ, 1, -1)] for c in range(3)]
            for t in range(count):
                spot = (t, slice(s * SUB, s * SUB + SUB), slice(None))
                link = [coef_ref[(k, *spot)] for k in range(7)]
                easy = [axis_ref[(c, *spot)] for c in range(3)]
                m = [here[c][t] for c in range(3)]
                project = easy[0] * m[0] + easy[1] * m[1] + easy[2] * m[2]
                h = []
                for c in range(3):
                    value = link[0] * rows_of(m_ref, (now, c), s, t, 1)
                    value = value + link[1] * rows_of(m_ref, (now, c), s, t, -1)
                    for k in range(4):
                        value = value + link[2 + k] * shifts[c][k](t)
                    value = value - link[6] * m[c]
                    h.append(value + project * easy[c] + applied[c])

                def cross(f, g):
                    return [
                        f[1] * g[2] - f[2] * g[1],
                        f[2] * g[0] - f[0] * g[2],
                        f[0] * g[1] - f[1] * g[0],
                    ]

                torque = cross(m, h)
                damped = cross(m, torque)
                moved = [
                    m[c] - (factor * torque[c] + (factor * DAMPING) * damped[c]) for c in range(3)
                ]
                size = moved[0] * moved[0] + moved[1] * moved[1] + moved[2] * moved[2]
                inverse = lax.rsqrt(size)
                for c in range(3):
                    store(m_ref, (later, c), s, t, moved[c] * inverse)
        return carry

    lax.fori_loop(0, STEPS, one_step, 0)

    last = STEPS % 2
    width_y = columns // NZ
    per = width_y // ngx
    row = iota((ngx * SUB, columns), 0)
    column = iota((ngx * SUB, columns), 1)
    cell = (row // SUB) * per + row % SUB
    inside = (column >= cell * NZ) & (column < cell * NZ + NZ) & (row % SUB < per)
    chooser = jnp.where(inside, 1.0, 0.0).astype(jnp.bfloat16)
    out_copy = pltpu.make_async_copy(moment_ref, moment_hbm, load.at[7])
    for c in range(3):
        for t in range(tiles):
            moment_ref[c, :, t * LANES : t * LANES + LANES] = m_ref[last, c, t, SUB : SUB + rows, :]
        whole = moment_ref[c]
        high = whole.astype(jnp.bfloat16)
        low = (whole - high.astype(jnp.float32)).astype(jnp.bfloat16)
        sums = sum(
            lax.dot_general(
                chooser, part, (((1,), (1,)), ((), ())), preferred_element_type=jnp.float32
            )
            for part in (low, high)
        )
        layer_ref[:, c * rows : c * rows + rows] = sums * (1.0 / math.sqrt(NZ))
    layer_ref[:, 3 * rows :] = jnp.zeros((ngx * SUB, rows), jnp.float32)

    def eight(index):
        return pl.ds(pl.multiple_of(index * SUB, SUB), SUB)

    mine = eight(gx)
    for k in range(1, ngx):
        other = wrap(gx + k, ngx)
        pltpu.make_async_remote_copy(
            src_ref=layer_ref.at[eight(other)], dst_ref=lines.at[mine],
            send_sem=send_x, recv_sem=recv_x, device_id=(other, gy), device_id_type=MESH,
        ).start()
    out_copy.start()
    lines[mine, :] = layer_ref[mine, :]
    rest = pl.ds(0, (ngx - 1) * SUB)
    pltpu.make_async_remote_copy(
        src_ref=layer_ref.at[rest], dst_ref=lines.at[rest], send_sem=send_x, recv_sem=recv_x,
        device_id=(wrap(gx + 1, ngx), gy), device_id_type=MESH,
    ).wait()
    loads[3].wait()
    loads[4].wait()
    whole = jnp.concatenate(
        [
            jnp.concatenate(
                [lines[s * SUB : s * SUB + SUB, c * rows : c * rows + rows] for s in range(ngx)],
                axis=1,
            )
            for c in range(3)
        ],
        axis=0,
    )
    waves = product(whole, xh, xl)
    per_x = rows // ngy
    wide = 2 * per_x
    blank = jnp.zeros((SUB, LANES - 3 * wide), jnp.float32)
    for d in range(devices):
        pieces = [waves[c * SUB : c * SUB + SUB, d * wide : d * wide + wide] for c in range(3)]
        message[d] = jnp.concatenate(pieces + [blank], axis=1)

    slot = gy * ngx + gx

    def give(other_x, other_y):
        pltpu.make_async_remote_copy(
            src_ref=message.at[other_x * ngy + other_y], dst_ref=held.at[slot],
            send_sem=send_y, recv_sem=recv_y, device_id=(other_x, other_y), device_id_type=MESH,
        ).start()

    for_others(ngx, ngy, gx, gy, give)
    held[slot] = message[gx * ngy + gy]
    loads[5].wait()
    loads[6].wait()
    rest = pl.ds(0, devices - 1)
    pltpu.make_async_remote_copy(
        src_ref=message.at[rest], dst_ref=held.at[rest], send_sem=send_y, recv_sem=recv_y,
        device_id=(wrap(gx + 1, ngx), gy), device_id_type=MESH,
    ).wait()
    table = held[...].reshape(devices * SUB, LANES).T
    total_y = yh.shape[1] // 2
    scale = 1.0 / math.sqrt(ngx * rows * total_y)
    spectrum = product(table, yh, yl) * scale
    for c in range(3):
        re = spectrum[c * wide : c * wide + per_x]
        im = spectrum[c * wide + per_x : c * wide + wide]
        spectrum_ref[c] = re[:, :total_y] + im[:, total_y:]
        spectrum_ref[3 + c] = im[:, :total_y] - re[:, total_y:]
    out_copy.wait()


def main(ngx, ngy, polar, azimuth, grains, tables, applied):
    rows, columns = polar.shape
    width_y = columns // NZ
    devices = ngx * ngy
    vmem, hbm = pl.BlockSpec(memory_space=pltpu.VMEM), pl.BlockSpec(memory_space=pl.ANY)
    strips, tiles = rows // SUB + 1, columns // LANES + 1
    waves = wave_tables(ngx, ngy, rows, width_y)
    messages = [(2, SUB, columns + columns // 2), (2, rows + rows // 2, LANES), (4, SUB, LANES)]
    floats = messages + messages + [
        (2, 3, tiles, SUB * (strips + 2), LANES),
        (tiles, SUB * (strips + 2), LANES),
        (7, tiles, SUB * strips, LANES),
        (3, tiles, SUB * strips, LANES),
        (3, rows, columns),
        (ngx * SUB, 4 * rows),
        (ngx * SUB, 4 * rows),
        (devices, SUB, LANES),
        (devices, SUB, LANES),
    ]
    dma = pltpu.SemaphoreType.DMA
    return pl.pallas_call(
        functools.partial(main_kernel, ngx, ngy),
        out_shape=[
            jax.ShapeDtypeStruct((3, rows, columns), jnp.float32),
            jax.ShapeDtypeStruct((6, rows // ngy, width_y * ngy), jnp.float32),
        ],
        in_specs=[hbm] * 7 + [vmem] * 4 + [pl.BlockSpec(memory_space=pltpu.SMEM)],
        out_specs=[hbm, vmem],
        scratch_shapes=[pltpu.VMEM(polar.shape, jnp.float32)] * 2
        + [pltpu.VMEM(polar.shape, jnp.int32)]
        + [pltpu.VMEM(t.shape, jnp.bfloat16) for t in waves]
        + [pltpu.VMEM(shape, jnp.float32) for shape in floats]
        + [dma((8,)), dma((8,)), dma((8,)), dma(()), dma(()), dma(()), dma(())],
        compiler_params=pltpu.CompilerParams(
            collective_id=0, has_side_effects=True, vmem_limit_bytes=60 * 2**20
        ),
        name="main",
    )(polar, azimuth, grains, *[jnp.asarray(t) for t in waves], *tables, applied)


def finish_kernel(ngx, ngy, spectrum_ref, moment_in, moment_out, flip_ref, non_ref, sem):
    copies = [
        pltpu.make_async_copy(moment_in.at[c], moment_out.at[c], sem.at[c]) for c in range(3)
    ]
    for copy in copies:
        copy.start()
    me = lax.axis_index("gx") * ngy + lax.axis_index("gy")
    per_x, total_y = flip_ref.shape
    total_x = per_x * ngx * ngy
    counter_x = me * per_x + iota((per_x, total_y), 0)
    counter_y = iota((per_x, total_y), 1)
    wave_x = jnp.where(counter_x < total_x // 2, counter_x, counter_x - total_x).astype(jnp.float32)
    wave_y = jnp.where(counter_y < total_y // 2, counter_y, counter_y - total_y).astype(jnp.float32)
    squared = wave_x * wave_x + wave_y * wave_y
    inverse = 1.0 / jnp.sqrt(jnp.maximum(squared, 1.0))
    beam_stop = jnp.where(squared > 0.5, 1.0, 0.0)
    unit_x, unit_y = wave_x * inverse, wave_y * inverse
    real = [spectrum_ref[c] for c in range(3)]
    imag = [spectrum_ref[3 + c] for c in range(3)]
    flip = jnp.zeros_like(squared)
    non = jnp.zeros_like(squared)
    for part in (real, imag):
        along = unit_x * part[0] + unit_y * part[1]
        first = part[0] - unit_x * along
        second = part[1] - unit_y * along
        non = non + first * first
        flip = flip + second * second + part[2] * part[2]
    flip_ref[...] = flip * beam_stop
    non_ref[...] = non * beam_stop
    for copy in copies:
        copy.wait()


def finish(ngx, ngy, spectrum, moment):
    vmem, hbm = pl.BlockSpec(memory_space=pltpu.VMEM), pl.BlockSpec(memory_space=pl.ANY)
    out = jax.ShapeDtypeStruct(spectrum.shape[1:], jnp.float32)
    return pl.pallas_call(
        functools.partial(finish_kernel, ngx, ngy),
        out_shape=[jax.ShapeDtypeStruct(moment.shape, jnp.float32), out, out],
        in_specs=[vmem, hbm],
        out_specs=[hbm, vmem, vmem],
        scratch_shapes=[pltpu.SemaphoreType.DMA((3,))],
        compiler_params=pltpu.CompilerParams(vmem_limit_bytes=60 * 2**20),
        name="finish",
    )(spectrum, moment)


def solution(mesh):
    ngx, ngy = mesh.shape["gx"], mesh.shape["gy"]

    def shards(polar, azimuth, grains, stiffness, anisotropy, axis_polar, axis_azimuth, applied):
        tables = [t.reshape(1, -1) for t in (stiffness, anisotropy, axis_polar, axis_azimuth)]
        moment, spectrum = main(ngx, ngy, polar, azimuth, grains, tables, applied)
        return tuple(finish(ngx, ngy, spectrum, moment))

    in_specs = (P("gx", "gy"), P("gx", "gy"), P("gx", "gy"), P(), P(), P(), P(), P())
    out_specs = (P(None, "gx", "gy"), P(("gx", "gy"), None), P(("gx", "gy"), None))
    return jax.shard_map(shards, mesh=mesh, in_specs=in_specs, out_specs=out_specs, check_vma=False)
```

```python
import functools
import math

import jax
import jax.numpy as jnp
import numpy as np
from jax import lax
from jax.experimental import pallas as pl
from jax.experimental.pallas import tpu as pltpu
from jax.sharding import PartitionSpec as P
import ml_dtypes

NZ = 12
STEPS = 4
DAMPING = 0.5
TIME_STEP = 0.12
LANES = 128
SUB = 8
MESH = pl.DeviceIdType.MESH


def iota(shape, dim):
    return lax.broadcasted_iota(jnp.int32, shape, dim)


def sin_cos(x):
    turns = jnp.floor(x * (2.0 / math.pi) + 0.5)
    quadrant = turns.astype(jnp.int32)
    r = x - turns * 1.5703125
    r = r - turns * 4.837512969970703125e-4
    r = r - turns * 7.549789948768648e-8
    z = r * r
    sine = r + r * z * (-1.6666654611e-1 + z * (8.3321608736e-3 - z * 1.9515295891e-4))
    cosine = 1.0 - 0.5 * z + z * z * (
        4.166664568298827e-2 + z * (-1.388731625493765e-3 + z * 2.443315711809948e-5)
    )
    odd = (quadrant & 1) == 1
    s = jnp.where(odd, cosine, sine)
    c = jnp.where(odd, sine, cosine)
    s = jnp.where((quadrant & 2) == 2, -s, s)
    c = jnp.where(((quadrant + 1) & 2) == 2, -c, c)
    return s, c


def wrap(value, count):
    return jnp.where(value >= count, value - count, value)


def for_others(ngx, ngy, gx, gy, act):
    def row(i, first):
        other_x = wrap(gx + i, ngx)
        for j in range(first, ngy):
            act(other_x, wrap(gy + j, ngy))

    def turn(i, carry):
        row(i, 0)
        return carry

    row(0, 1)
    lax.fori_loop(1, ngx, turn, 0)


def split(values):
    high = values.astype(ml_dtypes.bfloat16)
    low = (values - high.astype(np.float64)).astype(ml_dtypes.bfloat16)
    return high, low


def wave_tables(ngx, ngy, width_x, width_y):
    total_x, total_y = width_x * ngx, width_y * ngy
    devices = ngx * ngy
    per_x, per_y = width_x // ngy, width_y // ngx
    x = np.arange(total_x)
    angle = 2.0 * np.pi / total_x * (np.outer(x, x) % total_x)
    both = np.stack([np.cos(angle), -np.sin(angle)], axis=1).reshape(total_x, 2, devices, per_x)
    table_x = both.transpose(0, 2, 1, 3).reshape(total_x, 2 * total_x)
    y = np.arange(total_y)
    angle = 2.0 * np.pi / total_y * (np.outer(y, y) % total_y)
    both = np.concatenate([np.cos(angle), np.sin(angle)], axis=1)
    table_y = np.zeros((devices, SUB, 2 * total_y))
    table_y[:, :per_y] = both.reshape(devices, per_y, 2 * total_y)
    return (*split(table_x), *split(table_y.reshape(devices * SUB, 2 * total_y)))


def two_parts(value):
    high = value.astype(jnp.bfloat16).astype(jnp.float32)
    return jnp.concatenate([high, value - high], axis=0).astype(jnp.bfloat16)


def product(value, high_ref, low_ref):
    rows = value.shape[0]
    parts = two_parts(value)
    big = jnp.dot(parts, high_ref[...], preferred_element_type=jnp.float32)
    head = -(-rows // 16) * 16
    small = jnp.dot(parts[:head], low_ref[...], preferred_element_type=jnp.float32)
    return (big[rows:] + small[:rows]) + big[:rows]


def main_kernel(
    ngx, ngy, p_hbm, a_hbm, g_hbm, xh_hbm, xl_hbm, yh_hbm, yl_hbm,
    stiff_hbm, anis_hbm, apol_hbm, aazi_hbm, applied_ref, moment_ref, spectrum_ref,
    p_ref, a_ref, g_ref, xh, xl, yh, yl, stiff_ref, anis_ref, apol_ref, aazi_ref,
    rows_msg, cols_msg, corners_msg, rows_out, cols_out, corners_out,
    m_ref, w_ref, coef_ref, axis_ref, layer_ref, lines, message, held,
    load, send, recv, send_x, recv_x, send_y, recv_y,
):
    devices = ngx * ngy
    gx, gy = lax.axis_index("gx"), lax.axis_index("gy")
    down, up = wrap(gx + 1, ngx), wrap(gx + ngx - 1, ngx)
    right, left = wrap(gy + 1, ngy), wrap(gy + ngy - 1, ngy)
    around = [
        (up, gy), (down, gy), (gx, left), (gx, right),
        (up, left), (up, right), (down, left), (down, right),
    ]
    pairs = [
        (p_hbm, p_ref), (a_hbm, a_ref), (g_hbm, g_ref),
        (xh_hbm, xh), (xl_hbm, xl), (yh_hbm, yh), (yl_hbm, yl),
        (stiff_hbm, stiff_ref), (anis_hbm, anis_ref), (apol_hbm, apol_ref), (aazi_hbm, aazi_ref),
    ]
    loads = [pltpu.make_async_copy(s, t, load.at[k]) for k, (s, t) in enumerate(pairs)]
    for copy in loads[:3] + loads[7:]:
        copy.start()
    barrier = pltpu.get_barrier_semaphore()

    def greet(other_x, other_y):
        pl.semaphore_signal(barrier, inc=1, device_id=(other_x, other_y), device_id_type=MESH)

    for_others(ngx, ngy, gx, gy, greet)
    for copy in loads[:3]:
        copy.wait()

    rows, columns = p_ref.shape
    half = columns // 2
    near = (slice(0, SUB), slice(rows - SUB, rows))
    side = (slice(0, LANES), slice(columns - LANES, columns))
    sub_low = iota((SUB, columns), 0) < 4
    for k in range(2):
        own = sub_low if k == 0 else jnp.logical_not(sub_low)
        g = g_ref[near[k], :].astype(jnp.float32)
        rows_msg[k, :, :columns] = jnp.where(
            own, p_ref[near[k], :], pltpu.roll(a_ref[near[k], :], 4, 0)
        )
        rows_msg[k, :, columns:] = jnp.where(
            own[:, :half], g[:, :half], pltpu.roll(g[:, half:], 4, 0)
        )
    lane_low = iota((rows, LANES), 1) < 64
    for k in range(2):
        own = lane_low if k == 0 else jnp.logical_not(lane_low)
        g = g_ref[:, side[k]].astype(jnp.float32)
        cols_msg[k, :rows] = jnp.where(own, p_ref[:, side[k]], pltpu.roll(a_ref[:, side[k]], 64, 1))
        cols_msg[k, rows:] = jnp.where(
            own[: rows // 2], g[: rows // 2], pltpu.roll(g[rows // 2 :], 64, 1)
        )
    tile_sub = iota((SUB, LANES), 0) < 4
    tile_lane = iota((SUB, LANES), 1) < 64
    for k in range(2):
        for j in range(2):
            own_sub = tile_sub if k == 0 else jnp.logical_not(tile_sub)
            own_lane = tile_lane if j == 0 else jnp.logical_not(tile_lane)
            g = g_ref[near[k], side[j]].astype(jnp.float32)
            corners_msg[2 * k + j] = jnp.where(
                own_sub,
                jnp.where(own_lane, p_ref[near[k], side[j]], pltpu.roll(a_ref[near[k], side[j]], 64, 1)),
                pltpu.roll(g, 4, 0),
            )
    pl.semaphore_wait(barrier, devices - 1)
    sources = [rows_msg.at[0], rows_msg.at[1], cols_msg.at[0], cols_msg.at[1]]
    sources += [corners_msg.at[k] for k in range(4)]
    targets = [rows_out.at[0], rows_out.at[1], cols_out.at[0], cols_out.at[1]]
    targets += [corners_out.at[k] for k in range(4)]
    copies = [
        pltpu.make_async_remote_copy(
            src_ref=sources[k], dst_ref=targets[k], send_sem=send.at[k], recv_sem=recv.at[k],
            device_id=around[k], device_id_type=MESH,
        )
        for k in range(8)
    ]
    for copy in copies:
        copy.start()
    for copy in loads[3:7]:
        copy.start()
    for copy in loads[7:]:
        copy.wait()

    strips, tiles = rows // SUB, columns // LANES
    lane = iota((SUB, LANES), 1)
    sub = iota((SUB, LANES), 0)
    sub_low, lane_low = sub < 4, lane < 64

    def raw(s, t):
        if s < strips and t < tiles:
            r, c = slice(s * SUB, s * SUB + SUB), slice(t * LANES, t * LANES + LANES)
            return p_ref[r, c], a_ref[r, c], g_ref[r, c]
        if s < strips:
            r = slice(s * SUB, s * SUB + SUB)
            k = (s * SUB) % (rows // 2) + rows
            rg = slice(k, k + SUB)
            fr, fl = cols_out[0, r, :], cols_out[1, r, :]
            gr, gl = cols_out[0, rg, :], cols_out[1, rg, :]
            p = jnp.where(lane_low, fr, fl)
            a = pltpu.roll(jnp.where(lane_low, fl, fr), 64, 1)
            if s * SUB < rows // 2:
                g = jnp.where(lane_low, gr, gl)
            else:
                g = pltpu.roll(jnp.where(lane_low, gl, gr), 64, 1)
        elif t < tiles:
            c = slice(t * LANES, t * LANES + LANES)
            k = (t * LANES) % half + columns
            cg = slice(k, k + LANES)
            fn, fp = rows_out[0, :, c], rows_out[1, :, c]
            gn, gp = rows_out[0, :, cg], rows_out[1, :, cg]
            p = jnp.where(sub_low, fn, fp)
            a = pltpu.roll(jnp.where(sub_low, fp, fn), 4, 0)
            if t * LANES < half:
                g = jnp.where(sub_low, gn, gp)
            else:
                g = pltpu.roll(jnp.where(sub_low, gp, gn), 4, 0)
        else:
            q = [corners_out[k] for k in range(4)]
            p = jnp.where(sub_low, jnp.where(lane_low, q[0], q[1]), jnp.where(lane_low, q[2], q[3]))
            a = jnp.where(sub_low, jnp.where(lane_low, q[1], q[0]), jnp.where(lane_low, q[3], q[2]))
            a = pltpu.roll(a, 64, 1)
            g = jnp.where(sub_low, jnp.where(lane_low, q[2], q[3]), jnp.where(lane_low, q[0], q[1]))
            g = pltpu.roll(g, 4, 0)
        return p, a, g.astype(jnp.int32)

    def store(ref, lead, s, t, value):
        ref[(*lead, t, slice(SUB + s * SUB, 2 * SUB + s * SUB), slice(None))] = value
        if s == 0:
            k = SUB * (strips + 2)
            ref[(*lead, t, slice(k, k + SUB), slice(None))] = value
        if s == strips:
            ref[(*lead, t, slice(0, SUB), slice(None))] = value

    def rows_of(ref, lead, s, t, shift=0):
        k = SUB + s * SUB + shift
        return ref[(*lead, t, slice(k, k + SUB), slice(None))]

    sp, cp = sin_cos(apol_ref[...])
    sa, ca = sin_cos(aazi_ref[...])
    root = jnp.sqrt(anis_ref[...])
    tables = [stiff_ref[...], root * sp * ca, root * sp * sa, root * cp]
    pages = [
        [jnp.broadcast_to(table[:, k : k + LANES], (SUB, LANES)) for k in range(0, table.shape[1], LANES)]
        for table in tables
    ]

    def prepare(s, t):
        p, a, g = raw(s, t)
        sp, cp = sin_cos(p)
        sa, ca = sin_cos(a)
        for c, value in enumerate((sp * ca, sp * sa, cp)):
            store(m_ref, (0, c), s, t, value)
        place = g & (LANES - 1)
        page = g >> 7
        found = []
        for table in pages:
            value = jnp.take_along_axis(table[0], place, axis=1, mode="promise_in_bounds")
            for k in range(1, len(table)):
                other = jnp.take_along_axis(table[k], place, axis=1, mode="promise_in_bounds")
                value = jnp.where(page == k, other, value)
            found.append(value)
        store(w_ref, (), s, t, found[0])
        for c in range(3):
            axis_ref[c, t, s * SUB : s * SUB + SUB, :] = found[1 + c]

    for s in range(strips):
        for t in range(tiles):
            prepare(s, t)
    for copy in copies:
        copy.wait()
    for s in range(strips + 1):
        for t in range(tiles + 1):
            if s == strips or t == tiles:
                prepare(s, t)

    count = tiles + 1

    def shifter(values, shift):
        turned = {}

        def turn(t):
            t = t % count
            if t not in turned:
                turned[t] = pltpu.roll(values[t], (-shift) % LANES, 1)
            return turned[t]

        def at(t):
            if shift > 0:
                return jnp.where(lane < LANES - shift, turn(t), turn(t + 1))
            return jnp.where(lane >= -shift, turn(t), turn(t - 1))

        return at

    def couple(p, q):
        return 2.0 * p * q / (p + q)

    for s in range(strips + 1):
        here = [rows_of(w_ref, (), s, t) for t in range(count)]
        plus_y = shifter(here, NZ)
        plus_z = shifter(here, 1)
        y_link = [couple(here[t], plus_y(t)) for t in range(count)]
        z_link = []
        for t in range(count):
            spot = t * LANES + lane
            if t == tiles:
                spot = jnp.where(lane_low, spot, spot - count * LANES + NZ * LANES)
            level = spot - NZ * ((spot * 43691) >> 19)
            z_link.append(jnp.where(level < NZ - 1, couple(here[t], plus_z(t)), 0.0))
        y_back = shifter(y_link, -NZ)
        z_back = shifter(z_link, -1)
        for t in range(count):
            links = [
                couple(here[t], rows_of(w_ref, (), s, t, 1)),
                couple(here[t], rows_of(w_ref, (), s, t, -1)),
                y_link[t],
                y_back(t),
                z_link[t],
                z_back(t),
            ]
            total = links[0] + links[1] + links[2] + links[3] + links[4] + links[5]
            for k, value in enumerate(links + [total]):
                coef_ref[k, t, s * SUB : s * SUB + SUB, :] = value

    applied = [applied_ref[c] for c in range(3)]
    factor = TIME_STEP / (1.0 + DAMPING * DAMPING)

    def one_step(now, put, strip_count, tile_count):
        for s in range(strip_count):
            here = [[rows_of(m_ref, (now, c), s, t) for t in range(count)] for c in range(3)]
            shifts = [[shifter(here[c], k) for k in (NZ, -NZ, 1, -1)] for c in range(3)]
            for t in range(tile_count):
                spot = (t, slice(s * SUB, s * SUB + SUB), slice(None))
                link = [coef_ref[(k, *spot)] for k in range(7)]
                easy = [axis_ref[(c, *spot)] for c in range(3)]
                m = [here[c][t] for c in range(3)]
                project = easy[0] * m[0] + easy[1] * m[1] + easy[2] * m[2]
                h = []
                for c in range(3):
                    value = link[0] * rows_of(m_ref, (now, c), s, t, 1)
                    value = value + link[1] * rows_of(m_ref, (now, c), s, t, -1)
                    for k in range(4):
                        value = value + link[2 + k] * shifts[c][k](t)
                    value = value - link[6] * m[c]
                    h.append(value + project * easy[c] + applied[c])

                def cross(f, g):
                    return [
                        f[1] * g[2] - f[2] * g[1],
                        f[2] * g[0] - f[0] * g[2],
                        f[0] * g[1] - f[1] * g[0],
                    ]

                torque = cross(m, h)
                damped = cross(m, torque)
                moved = [
                    m[c] - (factor * torque[c] + (factor * DAMPING) * damped[c]) for c in range(3)
                ]
                size = moved[0] * moved[0] + moved[1] * moved[1] + moved[2] * moved[2]
                inverse = lax.rsqrt(size)
                for c in range(3):
                    put(c, s, t, moved[c] * inverse)

    def early_step(index, carry):
        now = lax.rem(index, 2)

        def put(c, s, t, value):
            store(m_ref, (1 - now, c), s, t, value)

        one_step(now, put, strips + 1, count)
        return carry

    def put_moment(c, s, t, value):
        moment_ref[c, s * SUB : s * SUB + SUB, t * LANES : t * LANES + LANES] = value

    lax.fori_loop(0, STEPS - 1, early_step, 0)
    one_step((STEPS - 1) % 2, put_moment, strips, tiles)

    width_y = columns // NZ
    per = width_y // ngx
    row = iota((ngx * SUB, columns), 0)
    column = iota((ngx * SUB, columns), 1)
    cell = (row // SUB) * per + row % SUB
    inside = (column >= cell * NZ) & (column < cell * NZ + NZ) & (row % SUB < per)
    chooser = jnp.where(inside, 1.0, 0.0).astype(jnp.bfloat16)
    for c in range(3):
        whole = moment_ref[c]
        high = whole.astype(jnp.bfloat16)
        low = (whole - high.astype(jnp.float32)).astype(jnp.bfloat16)
        sums = sum(
            lax.dot_general(
                chooser, part, (((1,), (1,)), ((), ())), preferred_element_type=jnp.float32
            )
            for part in (low, high)
        )
        layer_ref[:, c * rows : c * rows + rows] = sums * (1.0 / math.sqrt(NZ))
    layer_ref[:, 3 * rows :] = jnp.zeros((ngx * SUB, rows), jnp.float32)

    def eight(index):
        return pl.ds(pl.multiple_of(index * SUB, SUB), SUB)

    mine = eight(gx)
    for k in range(1, ngx):
        other = wrap(gx + k, ngx)
        pltpu.make_async_remote_copy(
            src_ref=layer_ref.at[eight(other)], dst_ref=lines.at[mine],
            send_sem=send_x, recv_sem=recv_x, device_id=(other, gy), device_id_type=MESH,
        ).start()
    lines[mine, :] = layer_ref[mine, :]
    rest = pl.ds(0, (ngx - 1) * SUB)
    pltpu.make_async_remote_copy(
        src_ref=layer_ref.at[rest], dst_ref=lines.at[rest], send_sem=send_x, recv_sem=recv_x,
        device_id=(wrap(gx + 1, ngx), gy), device_id_type=MESH,
    ).wait()
    loads[3].wait()
    loads[4].wait()
    whole = jnp.concatenate(
        [
            jnp.concatenate(
                [lines[s * SUB : s * SUB + SUB, c * rows : c * rows + rows] for s in range(ngx)],
                axis=1,
            )
            for c in range(3)
        ],
        axis=0,
    )
    waves = product(whole, xh, xl)
    per_x = rows // ngy
    wide = 2 * per_x
    blank = jnp.zeros((SUB, LANES - 3 * wide), jnp.float32)
    for d in range(devices):
        pieces = [waves[c * SUB : c * SUB + SUB, d * wide : d * wide + wide] for c in range(3)]
        message[d] = jnp.concatenate(pieces + [blank], axis=1)

    slot = gy * ngx + gx

    def give(other_x, other_y):
        pltpu.make_async_remote_copy(
            src_ref=message.at[other_x * ngy + other_y], dst_ref=held.at[slot],
            send_sem=send_y, recv_sem=recv_y, device_id=(other_x, other_y), device_id_type=MESH,
        ).start()

    for_others(ngx, ngy, gx, gy, give)
    held[slot] = message[gx * ngy + gy]
    loads[5].wait()
    loads[6].wait()
    rest = pl.ds(0, devices - 1)
    pltpu.make_async_remote_copy(
        src_ref=message.at[rest], dst_ref=held.at[rest], send_sem=send_y, recv_sem=recv_y,
        device_id=(wrap(gx + 1, ngx), gy), device_id_type=MESH,
    ).wait()
    table = held[...].reshape(devices * SUB, LANES).T
    total_y = yh.shape[1] // 2
    scale = 1.0 / math.sqrt(ngx * rows * total_y)
    spectrum = product(table, yh, yl) * scale
    for c in range(3):
        re = spectrum[c * wide : c * wide + per_x]
        im = spectrum[c * wide + per_x : c * wide + wide]
        spectrum_ref[c] = re[:, :total_y] + im[:, total_y:]
        spectrum_ref[3 + c] = im[:, :total_y] - re[:, total_y:]


def main(ngx, ngy, polar, azimuth, grains, tables, applied):
    rows, columns = polar.shape
    width_y = columns // NZ
    devices = ngx * ngy
    vmem, hbm = pl.BlockSpec(memory_space=pltpu.VMEM), pl.BlockSpec(memory_space=pltpu.HBM)
    strips, tiles = rows // SUB + 1, columns // LANES + 1
    waves = wave_tables(ngx, ngy, rows, width_y)
    messages = [(2, SUB, columns + columns // 2), (2, rows + rows // 2, LANES), (4, SUB, LANES)]
    floats = messages + messages + [
        (2, 3, tiles, SUB * (strips + 2), LANES),
        (tiles, SUB * (strips + 2), LANES),
        (7, tiles, SUB * strips, LANES),
        (3, tiles, SUB * strips, LANES),
        (ngx * SUB, 4 * rows),
        (ngx * SUB, 4 * rows),
        (devices, SUB, LANES),
        (devices, SUB, LANES),
    ]
    dma = pltpu.SemaphoreType.DMA

    def in_hbm(value):
        return pltpu.with_memory_space_constraint(jnp.asarray(value), pltpu.HBM)

    held_bytes = sum(2 * t.size for t in waves) + sum(4 * math.prod(f) for f in floats)
    room = min(60, 10 + held_bytes // 2**20)
    return pl.pallas_call(
        functools.partial(main_kernel, ngx, ngy),
        out_shape=[
            jax.ShapeDtypeStruct((3, rows, columns), jnp.float32),
            jax.ShapeDtypeStruct((6, rows // ngy, width_y * ngy), jnp.float32),
        ],
        in_specs=[hbm] * 11 + [pl.BlockSpec(memory_space=pltpu.SMEM)],
        out_specs=[vmem, vmem],
        scratch_shapes=[pltpu.VMEM(polar.shape, jnp.float32)] * 2
        + [pltpu.VMEM(polar.shape, jnp.int32)]
        + [pltpu.VMEM(t.shape, jnp.bfloat16) for t in waves]
        + [pltpu.VMEM(t.shape, jnp.float32) for t in tables]
        + [pltpu.VMEM(shape, jnp.float32) for shape in floats]
        + [dma((11,)), dma((8,)), dma((8,)), dma(()), dma(()), dma(()), dma(())],
        compiler_params=pltpu.CompilerParams(
            collective_id=0, has_side_effects=True, vmem_limit_bytes=room * 2**20
        ),
        name="main",
    )(*[in_hbm(t) for t in (polar, azimuth, grains, *waves, *tables, applied)])


def finish_kernel(ngx, ngy, spectrum_ref, moment_in, moment_out, flip_ref, non_ref, sem):
    rows = moment_in.shape[1]
    copies = []
    for c in range(3):
        for k in range(4):
            part = (c, pl.ds(k * (rows // 4), rows // 4))
            copies.append(
                pltpu.make_async_copy(moment_in.at[part], moment_out.at[part], sem.at[4 * c + k])
            )
    for copy in copies:
        copy.start()
    me = lax.axis_index("gx") * ngy + lax.axis_index("gy")
    per_x, total_y = flip_ref.shape
    total_x = per_x * ngx * ngy
    counter_x = me * per_x + iota((per_x, total_y), 0)
    counter_y = iota((per_x, total_y), 1)
    wave_x = jnp.where(counter_x < total_x // 2, counter_x, counter_x - total_x).astype(jnp.float32)
    wave_y = jnp.where(counter_y < total_y // 2, counter_y, counter_y - total_y).astype(jnp.float32)
    squared = wave_x * wave_x + wave_y * wave_y
    inverse = 1.0 / jnp.sqrt(jnp.maximum(squared, 1.0))
    beam_stop = jnp.where(squared > 0.5, 1.0, 0.0)
    unit_x, unit_y = wave_x * inverse, wave_y * inverse
    real = [spectrum_ref[c] for c in range(3)]
    imag = [spectrum_ref[3 + c] for c in range(3)]
    flip = jnp.zeros_like(squared)
    non = jnp.zeros_like(squared)
    for part in (real, imag):
        along = unit_x * part[0] + unit_y * part[1]
        first = part[0] - unit_x * along
        second = part[1] - unit_y * along
        non = non + first * first
        flip = flip + second * second + part[2] * part[2]
    flip_ref[...] = flip * beam_stop
    non_ref[...] = non * beam_stop
    for copy in copies:
        copy.wait()


def finish(ngx, ngy, spectrum, moment):
    vmem, hbm = pl.BlockSpec(memory_space=pltpu.VMEM), pl.BlockSpec(memory_space=pltpu.HBM)
    out = jax.ShapeDtypeStruct(spectrum.shape[1:], jnp.float32)
    return pl.pallas_call(
        functools.partial(finish_kernel, ngx, ngy),
        out_shape=[jax.ShapeDtypeStruct(moment.shape, jnp.float32), out, out],
        in_specs=[vmem, vmem],
        out_specs=[hbm, vmem, vmem],
        scratch_shapes=[pltpu.SemaphoreType.DMA((12,))],
        compiler_params=pltpu.CompilerParams(vmem_limit_bytes=8 * 2**20),
        name="finish",
    )(spectrum, moment)


def solution(mesh):
    ngx, ngy = mesh.shape["gx"], mesh.shape["gy"]

    def shards(polar, azimuth, grains, stiffness, anisotropy, axis_polar, axis_azimuth, applied):
        tables = [t.reshape(1, -1) for t in (stiffness, anisotropy, axis_polar, axis_azimuth)]
        moment, spectrum = main(ngx, ngy, polar, azimuth, grains, tables, applied)
        return tuple(finish(ngx, ngy, spectrum, moment))

    in_specs = (P("gx", "gy"), P("gx", "gy"), P("gx", "gy"), P(), P(), P(), P(), P())
    out_specs = (P(None, "gx", "gy"), P(("gx", "gy"), None), P(("gx", "gy"), None))
    return jax.shard_map(shards, mesh=mesh, in_specs=in_specs, out_specs=out_specs, check_vma=False)
```

```python
import functools
import math

import jax
import jax.numpy as jnp
import numpy as np
from jax import lax
from jax.experimental import pallas as pl
from jax.experimental.pallas import tpu as pltpu
from jax.sharding import PartitionSpec as P
import ml_dtypes

NZ = 12
STEPS = 4
DAMPING = 0.5
TIME_STEP = 0.12
LANES = 128
SUB = 8
MESH = pl.DeviceIdType.MESH


def iota(shape, dim):
    return lax.broadcasted_iota(jnp.int32, shape, dim)


def sin_cos(x):
    turns = jnp.floor(x * (2.0 / math.pi) + 0.5)
    quadrant = turns.astype(jnp.int32)
    r = x - turns * 1.5703125
    r = r - turns * 4.837512969970703125e-4
    r = r - turns * 7.549789948768648e-8
    z = r * r
    sine = r + r * z * (-1.6666654611e-1 + z * (8.3321608736e-3 - z * 1.9515295891e-4))
    cosine = 1.0 - 0.5 * z + z * z * (
        4.166664568298827e-2 + z * (-1.388731625493765e-3 + z * 2.443315711809948e-5)
    )
    odd = (quadrant & 1) == 1
    s = jnp.where(odd, cosine, sine)
    c = jnp.where(odd, sine, cosine)
    s = jnp.where((quadrant & 2) == 2, -s, s)
    c = jnp.where(((quadrant + 1) & 2) == 2, -c, c)
    return s, c


def wrap(value, count):
    return jnp.where(value >= count, value - count, value)


def for_others(ngx, ngy, gx, gy, act):
    def row(i, first):
        other_x = wrap(gx + i, ngx)
        for j in range(first, ngy):
            act(other_x, wrap(gy + j, ngy))

    def turn(i, carry):
        row(i, 0)
        return carry

    row(0, 1)
    lax.fori_loop(1, ngx, turn, 0)


def split(values):
    high = values.astype(ml_dtypes.bfloat16)
    low = (values - high.astype(np.float64)).astype(ml_dtypes.bfloat16)
    return high, low


def wave_tables(ngx, ngy, width_x, width_y):
    total_x, total_y = width_x * ngx, width_y * ngy
    devices = ngx * ngy
    per_x, per_y = width_x // ngy, width_y // ngx
    x = np.arange(total_x)
    angle = 2.0 * np.pi / total_x * (np.outer(x, x) % total_x)
    both = np.stack([np.cos(angle), -np.sin(angle)], axis=1).reshape(total_x, 2, devices, per_x)
    table_x = both.transpose(0, 2, 1, 3).reshape(total_x, 2 * total_x)
    y = np.arange(total_y)
    angle = 2.0 * np.pi / total_y * (np.outer(y, y) % total_y)
    both = np.concatenate([np.cos(angle), np.sin(angle)], axis=1)
    table_y = np.zeros((devices, SUB, 2 * total_y))
    table_y[:, :per_y] = both.reshape(devices, per_y, 2 * total_y)
    return (*split(table_x), *split(table_y.reshape(devices * SUB, 2 * total_y)))


def two_parts(value):
    high = value.astype(jnp.bfloat16).astype(jnp.float32)
    return jnp.concatenate([high, value - high], axis=0).astype(jnp.bfloat16)


def product(parts, high, low):
    rows = parts.shape[0] // 2
    big = jnp.dot(parts, high, preferred_element_type=jnp.float32)
    head = -(-rows // 16) * 16
    small = jnp.dot(parts[:head], low, preferred_element_type=jnp.float32)
    return (big[rows:] + small[:rows]) + big[:rows]


def main_kernel(
    ngx, ngy, p_hbm, a_hbm, g_hbm, xh_hbm, xl_hbm, yh_hbm, yl_hbm,
    stiff_hbm, anis_hbm, apol_hbm, aazi_hbm, applied_ref, moment_ref, spectrum_ref,
    p_ref, a_ref, g_ref, xh, xl, yh, yl, stiff_ref, anis_ref, apol_ref, aazi_ref,
    rows_msg, cols_msg, corners_msg, rows_out, cols_out, corners_out,
    m_ref, w_ref, coef_ref, axis_ref, layer_ref, lines, message, held,
    load, send, recv, send_x, recv_x, send_y, recv_y,
):
    devices = ngx * ngy
    gx, gy = lax.axis_index("gx"), lax.axis_index("gy")
    down, up = wrap(gx + 1, ngx), wrap(gx + ngx - 1, ngx)
    right, left = wrap(gy + 1, ngy), wrap(gy + ngy - 1, ngy)
    around = [
        (up, gy), (down, gy), (gx, left), (gx, right),
        (up, left), (up, right), (down, left), (down, right),
    ]
    pairs = [
        (p_hbm, p_ref), (a_hbm, a_ref), (g_hbm, g_ref),
        (xh_hbm, xh), (xl_hbm, xl), (yh_hbm, yh), (yl_hbm, yl),
        (stiff_hbm, stiff_ref), (anis_hbm, anis_ref), (apol_hbm, apol_ref), (aazi_hbm, aazi_ref),
    ]
    loads = [pltpu.make_async_copy(s, t, load.at[k]) for k, (s, t) in enumerate(pairs)]
    for copy in loads[:3] + loads[7:]:
        copy.start()
    barrier = pltpu.get_barrier_semaphore()

    def greet(other_x, other_y):
        pl.semaphore_signal(barrier, inc=1, device_id=(other_x, other_y), device_id_type=MESH)

    for_others(ngx, ngy, gx, gy, greet)
    for copy in loads[:3]:
        copy.wait()

    rows, columns = p_ref.shape
    half = columns // 2
    near = (slice(0, SUB), slice(rows - SUB, rows))
    side = (slice(0, LANES), slice(columns - LANES, columns))
    sub_low = iota((SUB, columns), 0) < 4
    for k in range(2):
        own = sub_low if k == 0 else jnp.logical_not(sub_low)
        g = g_ref[near[k], :].astype(jnp.float32)
        rows_msg[k, :, :columns] = jnp.where(
            own, p_ref[near[k], :], pltpu.roll(a_ref[near[k], :], 4, 0)
        )
        rows_msg[k, :, columns:] = jnp.where(
            own[:, :half], g[:, :half], pltpu.roll(g[:, half:], 4, 0)
        )
    lane_low = iota((rows, LANES), 1) < 64
    for k in range(2):
        own = lane_low if k == 0 else jnp.logical_not(lane_low)
        g = g_ref[:, side[k]].astype(jnp.float32)
        cols_msg[k, :rows] = jnp.where(own, p_ref[:, side[k]], pltpu.roll(a_ref[:, side[k]], 64, 1))
        cols_msg[k, rows:] = jnp.where(
            own[: rows // 2], g[: rows // 2], pltpu.roll(g[rows // 2 :], 64, 1)
        )
    tile_sub = iota((SUB, LANES), 0) < 4
    tile_lane = iota((SUB, LANES), 1) < 64
    for k in range(2):
        for j in range(2):
            own_sub = tile_sub if k == 0 else jnp.logical_not(tile_sub)
            own_lane = tile_lane if j == 0 else jnp.logical_not(tile_lane)
            g = g_ref[near[k], side[j]].astype(jnp.float32)
            corners_msg[2 * k + j] = jnp.where(
                own_sub,
                jnp.where(own_lane, p_ref[near[k], side[j]], pltpu.roll(a_ref[near[k], side[j]], 64, 1)),
                pltpu.roll(g, 4, 0),
            )
    pl.semaphore_wait(barrier, devices - 1)
    sources = [rows_msg.at[0], rows_msg.at[1], cols_msg.at[0], cols_msg.at[1]]
    sources += [corners_msg.at[k] for k in range(4)]
    targets = [rows_out.at[0], rows_out.at[1], cols_out.at[0], cols_out.at[1]]
    targets += [corners_out.at[k] for k in range(4)]
    copies = [
        pltpu.make_async_remote_copy(
            src_ref=sources[k], dst_ref=targets[k], send_sem=send.at[k], recv_sem=recv.at[k],
            device_id=around[k], device_id_type=MESH,
        )
        for k in range(8)
    ]
    for copy in copies:
        copy.start()
    for copy in loads[3:7]:
        copy.start()
    for copy in loads[7:]:
        copy.wait()

    strips, tiles = rows // SUB, columns // LANES
    lane = iota((SUB, LANES), 1)
    sub = iota((SUB, LANES), 0)
    sub_low, lane_low = sub < 4, lane < 64

    def raw(s, t):
        if s < strips and t < tiles:
            r, c = slice(s * SUB, s * SUB + SUB), slice(t * LANES, t * LANES + LANES)
            return p_ref[r, c], a_ref[r, c], g_ref[r, c]
        if s < strips:
            r = slice(s * SUB, s * SUB + SUB)
            k = (s * SUB) % (rows // 2) + rows
            rg = slice(k, k + SUB)
            fr, fl = cols_out[0, r, :], cols_out[1, r, :]
            gr, gl = cols_out[0, rg, :], cols_out[1, rg, :]
            p = jnp.where(lane_low, fr, fl)
            a = pltpu.roll(jnp.where(lane_low, fl, fr), 64, 1)
            if s * SUB < rows // 2:
                g = jnp.where(lane_low, gr, gl)
            else:
                g = pltpu.roll(jnp.where(lane_low, gl, gr), 64, 1)
        elif t < tiles:
            c = slice(t * LANES, t * LANES + LANES)
            k = (t * LANES) % half + columns
            cg = slice(k, k + LANES)
            fn, fp = rows_out[0, :, c], rows_out[1, :, c]
            gn, gp = rows_out[0, :, cg], rows_out[1, :, cg]
            p = jnp.where(sub_low, fn, fp)
            a = pltpu.roll(jnp.where(sub_low, fp, fn), 4, 0)
            if t * LANES < half:
                g = jnp.where(sub_low, gn, gp)
            else:
                g = pltpu.roll(jnp.where(sub_low, gp, gn), 4, 0)
        else:
            q = [corners_out[k] for k in range(4)]
            p = jnp.where(sub_low, jnp.where(lane_low, q[0], q[1]), jnp.where(lane_low, q[2], q[3]))
            a = jnp.where(sub_low, jnp.where(lane_low, q[1], q[0]), jnp.where(lane_low, q[3], q[2]))
            a = pltpu.roll(a, 64, 1)
            g = jnp.where(sub_low, jnp.where(lane_low, q[2], q[3]), jnp.where(lane_low, q[0], q[1]))
            g = pltpu.roll(g, 4, 0)
        return p, a, g.astype(jnp.int32)

    def store(ref, lead, s, t, value):
        ref[(*lead, t, slice(SUB + s * SUB, 2 * SUB + s * SUB), slice(None))] = value
        if s == 0:
            k = SUB * (strips + 2)
            ref[(*lead, t, slice(k, k + SUB), slice(None))] = value
        if s == strips:
            ref[(*lead, t, slice(0, SUB), slice(None))] = value

    def rows_of(ref, lead, s, t, shift=0):
        k = SUB + s * SUB + shift
        return ref[(*lead, t, slice(k, k + SUB), slice(None))]

    sp, cp = sin_cos(apol_ref[...])
    sa, ca = sin_cos(aazi_ref[...])
    root = jnp.sqrt(anis_ref[...])
    tables = [stiff_ref[...], root * sp * ca, root * sp * sa, root * cp]
    pages = [
        [jnp.broadcast_to(table[:, k : k + LANES], (SUB, LANES)) for k in range(0, table.shape[1], LANES)]
        for table in tables
    ]

    def prepare(s, t):
        p, a, g = raw(s, t)
        sp, cp = sin_cos(p)
        sa, ca = sin_cos(a)
        for c, value in enumerate((sp * ca, sp * sa, cp)):
            store(m_ref, (0, c), s, t, value)
        place = g & (LANES - 1)
        page = g >> 7
        found = []
        for table in pages:
            value = jnp.take_along_axis(table[0], place, axis=1, mode="promise_in_bounds")
            for k in range(1, len(table)):
                other = jnp.take_along_axis(table[k], place, axis=1, mode="promise_in_bounds")
                value = jnp.where(page == k, other, value)
            found.append(value)
        store(w_ref, (), s, t, found[0])
        for c in range(3):
            axis_ref[c, t, s * SUB : s * SUB + SUB, :] = found[1 + c]

    for s in range(strips):
        for t in range(tiles):
            prepare(s, t)
    for copy in copies:
        copy.wait()
    for s in range(strips + 1):
        for t in range(tiles + 1):
            if s == strips or t == tiles:
                prepare(s, t)

    count = tiles + 1

    def shifter(values, shift):
        turned = {}

        def turn(t):
            t = t % count
            if t not in turned:
                turned[t] = pltpu.roll(values[t], (-shift) % LANES, 1)
            return turned[t]

        def at(t):
            if shift > 0:
                return jnp.where(lane < LANES - shift, turn(t), turn(t + 1))
            return jnp.where(lane >= -shift, turn(t), turn(t - 1))

        return at

    def couple(p, q):
        return 2.0 * p * q / (p + q)

    for s in range(strips + 1):
        here = [rows_of(w_ref, (), s, t) for t in range(count)]
        plus_y = shifter(here, NZ)
        plus_z = shifter(here, 1)
        y_link = [couple(here[t], plus_y(t)) for t in range(count)]
        z_link = []
        for t in range(count):
            spot = t * LANES + lane
            if t == tiles:
                spot = jnp.where(lane_low, spot, spot - count * LANES + NZ * LANES)
            level = spot - NZ * ((spot * 43691) >> 19)
            z_link.append(jnp.where(level < NZ - 1, couple(here[t], plus_z(t)), 0.0))
        y_back = shifter(y_link, -NZ)
        z_back = shifter(z_link, -1)
        for t in range(count):
            links = [
                couple(here[t], rows_of(w_ref, (), s, t, 1)),
                couple(here[t], rows_of(w_ref, (), s, t, -1)),
                y_link[t],
                y_back(t),
                z_link[t],
                z_back(t),
            ]
            total = links[0] + links[1] + links[2] + links[3] + links[4] + links[5]
            for k, value in enumerate(links + [total]):
                coef_ref[k, t, s * SUB : s * SUB + SUB, :] = value

    applied = [applied_ref[c] for c in range(3)]
    factor = TIME_STEP / (1.0 + DAMPING * DAMPING)

    def one_step(now, put, strip_count, tile_count):
        for s in range(strip_count):
            here = [[rows_of(m_ref, (now, c), s, t) for t in range(count)] for c in range(3)]
            shifts = [[shifter(here[c], k) for k in (NZ, -NZ, 1, -1)] for c in range(3)]
            for t in range(tile_count):
                spot = (t, slice(s * SUB, s * SUB + SUB), slice(None))
                link = [coef_ref[(k, *spot)] for k in range(7)]
                easy = [axis_ref[(c, *spot)] for c in range(3)]
                m = [here[c][t] for c in range(3)]
                project = easy[0] * m[0] + easy[1] * m[1] + easy[2] * m[2]
                h = []
                for c in range(3):
                    value = link[0] * rows_of(m_ref, (now, c), s, t, 1)
                    value = value + link[1] * rows_of(m_ref, (now, c), s, t, -1)
                    for k in range(4):
                        value = value + link[2 + k] * shifts[c][k](t)
                    value = value - link[6] * m[c]
                    h.append(value + project * easy[c] + applied[c])

                def cross(f, g):
                    return [
                        f[1] * g[2] - f[2] * g[1],
                        f[2] * g[0] - f[0] * g[2],
                        f[0] * g[1] - f[1] * g[0],
                    ]

                torque = cross(m, h)
                damped = cross(m, torque)
                moved = [
                    m[c] - (factor * torque[c] + (factor * DAMPING) * damped[c]) for c in range(3)
                ]
                size = moved[0] * moved[0] + moved[1] * moved[1] + moved[2] * moved[2]
                inverse = lax.rsqrt(size)
                for c in range(3):
                    put(c, s, t, moved[c] * inverse)

    def early_step(index, carry):
        now = lax.rem(index, 2)

        def put(c, s, t, value):
            store(m_ref, (1 - now, c), s, t, value)

        one_step(now, put, strips + 1, count)
        return carry

    def put_moment(c, s, t, value):
        moment_ref[c, s * SUB : s * SUB + SUB, t * LANES : t * LANES + LANES] = value

    lax.fori_loop(0, STEPS - 1, early_step, 0)
    one_step((STEPS - 1) % 2, put_moment, strips, tiles)

    width_y = columns // NZ
    per = width_y // ngx
    row = iota((ngx * SUB, columns), 0)
    column = iota((ngx * SUB, columns), 1)
    cell = (row // SUB) * per + row % SUB
    inside = (column >= cell * NZ) & (column < cell * NZ + NZ) & (row % SUB < per)
    chooser = jnp.where(inside, 1.0, 0.0).astype(jnp.bfloat16)
    for c in range(3):
        whole = moment_ref[c]
        high = whole.astype(jnp.bfloat16)
        low = (whole - high.astype(jnp.float32)).astype(jnp.bfloat16)
        sums = sum(
            lax.dot_general(
                chooser, part, (((1,), (1,)), ((), ())), preferred_element_type=jnp.float32
            )
            for part in (low, high)
        )
        layer_ref[:, c * rows : c * rows + rows] = sums * (1.0 / math.sqrt(NZ))
    layer_ref[:, 3 * rows :] = jnp.zeros((ngx * SUB, rows), jnp.float32)

    def eight(index):
        return pl.ds(pl.multiple_of(index * SUB, SUB), SUB)

    mine = eight(gx)
    for k in range(1, ngx):
        other = wrap(gx + k, ngx)
        pltpu.make_async_remote_copy(
            src_ref=layer_ref.at[eight(other)], dst_ref=lines.at[mine],
            send_sem=send_x, recv_sem=recv_x, device_id=(other, gy), device_id_type=MESH,
        ).start()
    lines[mine, :] = layer_ref[mine, :]
    rest = pl.ds(0, (ngx - 1) * SUB)
    pltpu.make_async_remote_copy(
        src_ref=layer_ref.at[rest], dst_ref=lines.at[rest], send_sem=send_x, recv_sem=recv_x,
        device_id=(wrap(gx + 1, ngx), gy), device_id_type=MESH,
    ).wait()
    loads[3].wait()
    loads[4].wait()
    whole = jnp.concatenate(
        [
            jnp.concatenate(
                [lines[s * SUB : s * SUB + SUB, c * rows : c * rows + rows] for s in range(ngx)],
                axis=1,
            )
            for c in range(3)
        ],
        axis=0,
    )
    per_x = rows // ngy
    wide = 2 * per_x
    blank = jnp.zeros((SUB, LANES - 3 * wide), jnp.float32)
    slot = gy * ngx + gx

    parts = two_parts(whole)
    for k in [*range(1, ngx), 0]:
        other_x = wrap(gx + k, ngx)
        lanes = pl.ds(pl.multiple_of(other_x * (wide * ngy), LANES), wide * ngy)
        chunk = product(parts, xh[:, lanes], xl[:, lanes])
        for j in range(ngy):
            pieces = [chunk[c * SUB : c * SUB + SUB, j * wide : j * wide + wide] for c in range(3)]
            message[other_x * ngy + j] = jnp.concatenate(pieces + [blank], axis=1)
        for j in range(0 if k else 1, ngy):
            other_y = wrap(gy + j, ngy)
            pltpu.make_async_remote_copy(
                src_ref=message.at[other_x * ngy + other_y], dst_ref=held.at[slot],
                send_sem=send_y, recv_sem=recv_y, device_id=(other_x, other_y),
                device_id_type=MESH,
            ).start()

    held[slot] = message[gx * ngy + gy]
    loads[5].wait()
    loads[6].wait()
    rest = pl.ds(0, devices - 1)
    pltpu.make_async_remote_copy(
        src_ref=message.at[rest], dst_ref=held.at[rest], send_sem=send_y, recv_sem=recv_y,
        device_id=(wrap(gx + 1, ngx), gy), device_id_type=MESH,
    ).wait()
    table = held[...].reshape(devices * SUB, LANES).T
    total_y = yh.shape[1] // 2
    scale = 1.0 / math.sqrt(ngx * rows * total_y)
    spectrum = product(two_parts(table), yh[...], yl[...]) * scale
    for c in range(3):
        re = spectrum[c * wide : c * wide + per_x]
        im = spectrum[c * wide + per_x : c * wide + wide]
        spectrum_ref[c] = re[:, :total_y] + im[:, total_y:]
        spectrum_ref[3 + c] = im[:, :total_y] - re[:, total_y:]


def main(ngx, ngy, polar, azimuth, grains, tables, applied):
    rows, columns = polar.shape
    width_y = columns // NZ
    devices = ngx * ngy
    vmem, hbm = pl.BlockSpec(memory_space=pltpu.VMEM), pl.BlockSpec(memory_space=pltpu.HBM)
    strips, tiles = rows // SUB + 1, columns // LANES + 1
    waves = wave_tables(ngx, ngy, rows, width_y)
    messages = [(2, SUB, columns + columns // 2), (2, rows + rows // 2, LANES), (4, SUB, LANES)]
    floats = messages + messages + [
        (2, 3, tiles, SUB * (strips + 2), LANES),
        (tiles, SUB * (strips + 2), LANES),
        (7, tiles, SUB * strips, LANES),
        (3, tiles, SUB * strips, LANES),
        (ngx * SUB, 4 * rows),
        (ngx * SUB, 4 * rows),
        (devices, SUB, LANES),
        (devices, SUB, LANES),
    ]
    dma = pltpu.SemaphoreType.DMA

    def in_hbm(value):
        return pltpu.with_memory_space_constraint(jnp.asarray(value), pltpu.HBM)

    held_bytes = sum(2 * t.size for t in waves) + sum(4 * math.prod(f) for f in floats)
    room = min(60, 10 + held_bytes // 2**20)
    return pl.pallas_call(
        functools.partial(main_kernel, ngx, ngy),
        out_shape=[
            jax.ShapeDtypeStruct((3, rows, columns), jnp.float32),
            jax.ShapeDtypeStruct((6, rows // ngy, width_y * ngy), jnp.float32),
        ],
        in_specs=[hbm] * 11 + [pl.BlockSpec(memory_space=pltpu.SMEM)],
        out_specs=[vmem, vmem],
        scratch_shapes=[pltpu.VMEM(polar.shape, jnp.float32)] * 2
        + [pltpu.VMEM(polar.shape, jnp.int32)]
        + [pltpu.VMEM(t.shape, jnp.bfloat16) for t in waves]
        + [pltpu.VMEM(t.shape, jnp.float32) for t in tables]
        + [pltpu.VMEM(shape, jnp.float32) for shape in floats]
        + [dma((11,)), dma((8,)), dma((8,)), dma(()), dma(()), dma(()), dma(())],
        compiler_params=pltpu.CompilerParams(
            collective_id=0, has_side_effects=True, vmem_limit_bytes=room * 2**20
        ),
        name="main",
    )(*[in_hbm(t) for t in (polar, azimuth, grains, *waves, *tables, applied)])


def finish_kernel(ngx, ngy, spectrum_ref, moment_in, moment_out, flip_ref, non_ref, sem):
    rows = moment_in.shape[1]
    copies = []
    for c in range(3):
        for k in range(4):
            part = (c, pl.ds(k * (rows // 4), rows // 4))
            copies.append(
                pltpu.make_async_copy(moment_in.at[part], moment_out.at[part], sem.at[4 * c + k])
            )
    for copy in copies:
        copy.start()
    me = lax.axis_index("gx") * ngy + lax.axis_index("gy")
    per_x, total_y = flip_ref.shape
    total_x = per_x * ngx * ngy
    counter_x = me * per_x + iota((per_x, total_y), 0)
    counter_y = iota((per_x, total_y), 1)
    wave_x = jnp.where(counter_x < total_x // 2, counter_x, counter_x - total_x).astype(jnp.float32)
    wave_y = jnp.where(counter_y < total_y // 2, counter_y, counter_y - total_y).astype(jnp.float32)
    squared = wave_x * wave_x + wave_y * wave_y
    inverse = 1.0 / jnp.sqrt(jnp.maximum(squared, 1.0))
    beam_stop = jnp.where(squared > 0.5, 1.0, 0.0)
    unit_x, unit_y = wave_x * inverse, wave_y * inverse
    real = [spectrum_ref[c] for c in range(3)]
    imag = [spectrum_ref[3 + c] for c in range(3)]
    flip = jnp.zeros_like(squared)
    non = jnp.zeros_like(squared)
    for part in (real, imag):
        along = unit_x * part[0] + unit_y * part[1]
        first = part[0] - unit_x * along
        second = part[1] - unit_y * along
        non = non + first * first
        flip = flip + second * second + part[2] * part[2]
    flip_ref[...] = flip * beam_stop
    non_ref[...] = non * beam_stop
    for copy in copies:
        copy.wait()


def finish(ngx, ngy, spectrum, moment):
    vmem, hbm = pl.BlockSpec(memory_space=pltpu.VMEM), pl.BlockSpec(memory_space=pltpu.HBM)
    out = jax.ShapeDtypeStruct(spectrum.shape[1:], jnp.float32)
    return pl.pallas_call(
        functools.partial(finish_kernel, ngx, ngy),
        out_shape=[jax.ShapeDtypeStruct(moment.shape, jnp.float32), out, out],
        in_specs=[vmem, vmem],
        out_specs=[hbm, vmem, vmem],
        scratch_shapes=[pltpu.SemaphoreType.DMA((12,))],
        compiler_params=pltpu.CompilerParams(vmem_limit_bytes=8 * 2**20),
        name="finish",
    )(spectrum, moment)


def solution(mesh):
    ngx, ngy = mesh.shape["gx"], mesh.shape["gy"]

    def shards(polar, azimuth, grains, stiffness, anisotropy, axis_polar, axis_azimuth, applied):
        tables = [t.reshape(1, -1) for t in (stiffness, anisotropy, axis_polar, axis_azimuth)]
        moment, spectrum = main(ngx, ngy, polar, azimuth, grains, tables, applied)
        return tuple(finish(ngx, ngy, spectrum, moment))

    in_specs = (P("gx", "gy"), P("gx", "gy"), P("gx", "gy"), P(), P(), P(), P(), P())
    out_specs = (P(None, "gx", "gy"), P(("gx", "gy"), None), P(("gx", "gy"), None))
    return jax.shard_map(shards, mesh=mesh, in_specs=in_specs, out_specs=out_specs, check_vma=False)
```
